512 devices in a mesh: group: 4 (over z_hi), seq: 16 (over y, core), dp: 8 (over x, z_lo).
Axes of the slice: x: 4, y: 8, z: 8 (z_hi: 4, z_lo: 2; z = z_hi * 2 + z_lo), core: 2. Of those that a mesh axis runs over, the one named last changes fastest.
Arguments:
- noise_gen: bfloat16 [16, 1024, 64], P('dp', 'seq'), may hold values from -6 to 6
- noise_score: bfloat16 [16, 1024, 64], P('dp', 'seq'), may hold values from -6 to 6
- prev_latents: float32 [16, 1024, 64], P('dp', 'seq'), may hold values from -42 to 42
- t_idx: int32 [16], P('dp'), may hold values from 0 to 999
- w_in: bfloat16 [4, 64, 3072], P('group'), may hold values from -4 to 4, as said below
- w_qkv: bfloat16 [4, 3072, 3, 2048], P('group', None, None, 'seq'), may hold values from -4 to 4, as said below
- w_out: bfloat16 [4, 2048, 64], P('group', 'seq'), may hold values from -4 to 4, as said below
- w_final: bfloat16 [4, 3072, 64], P('group'), may hold values from -4 to 4, as said below
- mod_scale: float32 [4, 3072], P('group'), may hold values from -0.5 to 0.5
- mod_shift: float32 [4, 3072], P('group'), may hold values from -3 to 3
- saved_features: bfloat16 [16, 1024, 3072], P('dp', 'seq'), may hold values from -6 to 6
Outputs:
- predictions: float32 [4, 16, 1024, 64], P('group', 'dp', 'seq')
- dmd_grad: float32 [16, 1024, 64], P('dp', 'seq')
- gen_final_grad: float32 [3072, 64], replicated
The draws below stay inside these ranges and needn't reach their ends.
Inputs may be any that keep to these rules, and one draw needn't show every extreme that they name: `w_in`: groups 1 and 2 hold equal weights. `w_qkv`: groups 1 and 2 hold equal weights. `w_out`: groups 1 and 2 hold equal weights. `w_final`: groups 1 and 2 hold equal weights.
All inputs are finite; a program needn't handle non-finite values. Where the reference program divides by a largest or mean magnitude, that divisor is 1e-20 or more.
Results may differ from the reference program's by a relative error of at most 0.017.
Values may be sent and summed in bfloat16 or wider, within the bound.
No kernel may reach another device: no remote copies, remote signals or barrier semaphores. Data moves between devices by JAX's collectives and lax.ppermute only.
A program may use at most 128 MiB of HBM per device.

```python
import math
import jax
import jax.numpy as jnp
from jax import lax

D = 3072
HD = 128
PATCH = 64
NTOK = 1024
NOISE_LEVEL_COUNT = 1000
HEADS = 16
IMAGES = 16


def grouped(key, shape, fan):
    base = jnp.clip(jax.random.normal(key, (3,) + shape, jnp.float32), -4.0, 4.0) * fan ** (-0.5)
    return jnp.stack([base[0], base[1], base[1], base[2]]).astype(jnp.bfloat16)


def draw_w_in(key, part):
    key = jax.random.fold_in(key, 21)
    return grouped(key, (PATCH, D), PATCH)


def draw_w_qkv(key, part):
    key = jax.random.fold_in(key, 22)
    return grouped(key, (D, 3, HEADS * HD), D)


def draw_w_out(key, part):
    key = jax.random.fold_in(key, 23)
    return grouped(key, (HEADS * HD, PATCH), HEADS * HD)


def draw_w_final(key, part):
    key = jax.random.fold_in(key, 24)
    return grouped(key, (D, PATCH), D)


def draw_prev_latents(key, part):
    key = jax.random.fold_in(key, 25)
    first, second_operand = jax.random.split(key)
    token_position = jnp.arange(NTOK, dtype=jnp.float32) / NTOK
    rough = jnp.exp(jax.random.uniform(second_operand, (IMAGES, NTOK, 1), jnp.float32, 0.0, math.log(3.5)))
    factor = 3.0 ** token_position[None, :, None] * rough
    base = jnp.clip(jax.random.normal(first, (IMAGES, NTOK, PATCH), jnp.float32), -4.0, 4.0)
    return base * factor


def touch_ends(values, key, smallest, largest):
    index_at = [jax.random.randint(jax.random.fold_in(key, axis), (), 0, length) for axis, length in enumerate(values.shape)]
    longest = values.shape.index(max(values.shape))
    neighbour = index_at[:longest] + [(index_at[longest] + 1) % values.shape[longest]] + index_at[longest + 1:]
    return values.at[tuple(index_at)].set(smallest).at[tuple(neighbour)].set(largest)


def block_scale(stream_key, dims, pieces, least, largest):
    loudness = 1.0
    for axis_at, shards_of in pieces:
        heights = jax.random.uniform(jax.random.fold_in(jax.random.fold_in(stream_key, 6), axis_at), (shards_of,), jnp.float32, least / len(pieces), largest / len(pieces))
        loudness = loudness * jnp.repeat(jnp.exp(heights), dims[axis_at] // shards_of).reshape((-1,) + (1,) * (len(dims) - 1 - axis_at))
    return loudness


def noise(key, shape, deviation, limit, cuts=(), kind=jnp.bfloat16):
    array = jax.random.normal(key, shape, jnp.float32) * deviation
    if len(cuts) > 0:
        array = block_scale(key, shape, cuts, -0.22, 0.18) * array
    return jnp.clip(array, min=-limit, max=limit).astype(kind)


def setup_inputs(seed: int = 0) -> dict:
    splits = jax.random.split(jax.random.key(seed), 12)
    noise_gen = noise(splits[0], (IMAGES, NTOK, PATCH), 1.0, 6.0, ((0, 8), (1, 16)))
    noise_score = noise(splits[1], (IMAGES, NTOK, PATCH), 1.0, 6.0, ((0, 8), (1, 16)))
    prev_latents = draw_prev_latents(jax.random.fold_in(splits[11], 71), 0)
    t_idx = touch_ends(jax.random.randint(splits[3], (IMAGES,), 0, NOISE_LEVEL_COUNT), jax.random.fold_in(splits[3], 1), 0, NOISE_LEVEL_COUNT - 1).astype(jnp.int32)
    w_in = draw_w_in(jax.random.fold_in(splits[11], 71), 0)
    w_qkv = draw_w_qkv(jax.random.fold_in(splits[11], 71), 0)
    w_out = draw_w_out(jax.random.fold_in(splits[11], 71), 0)
    w_final = draw_w_final(jax.random.fold_in(splits[11], 71), 0)
    mod_scale = jnp.clip(jax.random.uniform(splits[8], (4, D), jnp.float32, -0.5, 0.5) * block_scale(splits[8], (4, D), ((0, 4),), -0.4, 0.0), -0.5, 0.5)
    mod_shift = noise(splits[9], (4, D), 0.5, 3.0, ((0, 4),), jnp.float32)
    saved_features = noise(splits[10], (IMAGES, NTOK, D), 1.0, 6.0, ((0, 8), (1, 16)))
    return {"noise_gen": noise_gen, "noise_score": noise_score, "prev_latents": prev_latents, "t_idx": t_idx, "w_in": w_in, "w_qkv": w_qkv, "w_out": w_out, "w_final": w_final, "mod_scale": mod_scale, "mod_shift": mod_shift, "saved_features": saved_features}


def rounded(value_rows):
    return lax.optimization_barrier(value_rows.astype(jnp.bfloat16)).astype(jnp.float32)

def model_pass(model_input, noise_level, w_in, w_qkv, w_out, w_final, scale, shift):
    projected = jnp.einsum('inp,pd->ind', model_input.astype(jnp.bfloat16).astype(jnp.float32), w_in.astype(jnp.float32))
    normed = projected * lax.rsqrt(lax.optimization_barrier(jnp.mean(projected * projected, axis=-1, keepdims=True)) + 1e-06)
    features = rounded(normed * (1.0 + noise_level[:, None, None] * scale) + shift)
    head_weights = w_qkv.reshape(D, 3, HEADS, HD).transpose(2, 0, 1, 3)
    head_maps = w_out.reshape(HEADS, HD, PATCH)

    def one_head(pair):
        weight, output_layout = pair
        triple = rounded(jnp.einsum('ind,dce->cine', features, weight.astype(jnp.float32)))
        scores = jnp.einsum('iqe,ike->iqk', triple[0], triple[1]) / math.sqrt(HD)
        probs = rounded(jax.nn.softmax(scores, axis=-1))
        attention_result = rounded(jnp.einsum('iqk,ike->iqe', probs, triple[2]))
        return jnp.einsum('iqe,ep->iqp', attention_result, output_layout.astype(jnp.float32))
    terms = lax.map(one_head, (head_weights, head_maps))
    local = jnp.einsum('ind,dp->inp', features, w_final.astype(jnp.float32))
    return local + lax.optimization_barrier(jnp.sum(terms, axis=0))

def reference(noise_gen, noise_score, prev_latents, t_idx, w_in, w_qkv, w_out, w_final, mod_scale, mod_shift, saved_features):
    level = (t_idx.astype(jnp.float32) + 0.5) / NOISE_LEVEL_COUNT
    noisy = (1.0 - level)[:, None, None] * prev_latents + level[:, None, None] * noise_score.astype(jnp.float32)
    outputs = []
    for index in range(4):
        if index == 0:
            model_input = noise_gen.astype(jnp.float32)
            noise_level = jnp.ones_like(level)
        else:
            model_input = noisy
            noise_level = level
        velocity = model_pass(model_input, noise_level, w_in[index], w_qkv[index], w_out[index], w_final[index], mod_scale[index], mod_shift[index])
        outputs.append(model_input - noise_level[:, None, None] * velocity)
    real = outputs[2] + 2.5 * (outputs[1] - outputs[2])
    fake = outputs[3]
    spread = lax.optimization_barrier(jnp.mean(jnp.abs(prev_latents - real), axis=(1, 2))) + 1e-05
    dmd_grad = (fake - real) / spread[:, None, None]
    down = (-dmd_grad).astype(jnp.bfloat16).astype(jnp.float32)
    total = jnp.einsum('ind,inp->dp', saved_features.astype(jnp.float32), down)
    gen_final_grad = total / math.sqrt(IMAGES * NTOK)
    return (jnp.stack(outputs), dmd_grad, gen_final_grad)
```

```python
import math

import jax
import jax.numpy as jnp
from jax import lax
from jax.experimental import pallas as pl
from jax.experimental.pallas import tpu as pltpu
from jax.sharding import PartitionSpec as P

NTOK = 1024
NOISE_LEVEL_COUNT = 1000
BF16 = jnp.bfloat16
F32 = jnp.float32
ROWS = 208


def dot(a, b, lhs=1, rhs=0):
    return lax.dot_general(a, b, (((lhs,), (rhs,)), ((), ())), preferred_element_type=F32)


def left_half(shape):
    return lax.broadcasted_iota(jnp.int32, shape, 1) < 64


def levels(group_ref, t_ref):
    gen = jnp.where(group_ref[0] == 0, 1.0, 0.0).astype(F32)
    level = [(t_ref[i].astype(F32) + 0.5) * (1.0 / NOISE_LEVEL_COUNT) for i in range(2)]
    return gen, level, [gen + (1.0 - gen) * value for value in level]


def noisy_latent(level, prev, noise):
    return (1.0 - level) * prev + level * noise.astype(F32)


def fold_kernel(
    group_ref, t_ref, gen_ref, noise_ref, prev_ref, w_in_ref, w_qkv_ref, w_out_ref, w_final_ref,
    scale_ref, shift_ref, sent_ref, local_ref, left_ref,
):
    width = w_in_ref.shape[2]
    gen, level, used = levels(group_ref, t_ref)
    latents = []
    for i in range(2):
        noisy = noisy_latent(level[i], prev_ref[i], noise_ref[i])
        latents.append(gen * gen_ref[i].astype(F32) + (1.0 - gen) * noisy)
    latent = jnp.concatenate(latents, axis=0).astype(BF16)
    step = 512
    squares = jnp.zeros((128, step), F32)
    for at in range(0, width, step):
        part = w_in_ref[0, :, at : at + step]
        projected = dot(latent, part)
        squares = squares + projected * projected
        scale = scale_ref[:, at : at + step]
        shift = shift_ref[:, at : at + step]
        high = shift.astype(BF16).astype(F32)
        row = lax.broadcasted_iota(jnp.int32, (16, step), 0)
        left_ref[0:64, at : at + step] = part
        left_ref[64:128, at : at + step] = (part.astype(F32) * scale).astype(BF16)
        left_ref[128:144, at : at + step] = jnp.where(
            row == 0, high, jnp.where(row == 1, shift - high, 0.0)
        ).astype(BF16)
    mean = jnp.sum(squares, axis=1, keepdims=True) * (1.0 / width)
    scaled = (latent.astype(F32) * lax.rsqrt(mean + 1e-06)).astype(BF16)
    sent_ref[144:208, :] = jnp.concatenate([scaled[0:64], scaled[64:128]], axis=1)

    folded = [dot(left_ref[...], w_qkv_ref[c]) for c in range(3)]
    final = dot(left_ref[...], w_final_ref[...], 1, 1)
    const = [part[128:129] + part[129:130] for part in folded]
    final_const = final[128:129] + final[129:130]
    factor = math.log2(math.e) / math.sqrt(128.0)
    w_out = w_out_ref[...]
    blocks, consts, locals_ = [], [], []
    value_const = dot(jnp.broadcast_to(const[2], (16, 128)).astype(BF16), w_out, 1, 1)
    for i in range(2):
        q, k, v = [(part[0:64] + used[i] * part[64:128]) for part in folded]
        kb = k.astype(BF16)
        scores = dot(q.astype(BF16), kb, 1, 1) * factor
        out = dot(v.astype(BF16), w_out, 1, 1)
        key_const = dot(jnp.broadcast_to(const[0], (16, 128)).astype(BF16), kb, 1, 1) * factor
        local = final[0:64] + used[i] * final[64:128]
        zero = jnp.zeros_like(local)
        if i == 0:
            blocks.append(jnp.concatenate([scores, out], axis=1))
            consts.append(jnp.concatenate([key_const, value_const], axis=1))
            locals_.append(jnp.concatenate([zero, local], axis=1))
        else:
            blocks.append(jnp.concatenate([out, scores], axis=1))
            consts.append(jnp.concatenate([value_const, key_const], axis=1))
            locals_.append(jnp.concatenate([local, zero], axis=1))
    sent_ref[0:64, :] = blocks[0].astype(BF16)
    sent_ref[64:128, :] = blocks[1].astype(BF16)
    row = lax.broadcasted_iota(jnp.int32, (16, 128), 0)
    sent_ref[128:144, :] = jnp.where(row == 0, consts[0], consts[1]).astype(BF16)
    local_ref[0:64, :] = locals_[0]
    local_ref[64:128, :] = locals_[1]
    both = jnp.concatenate([final_const, final_const], axis=1)
    local_ref[128:136, :] = jnp.broadcast_to(both, (8, 128))


def attend_kernel(
    group_ref, t_ref, gen_ref, noise_ref, prev_ref, all_ref, own_ref, local_ref,
    moved_ref, prediction_ref, keys_ref, query_ref, mixed_ref,
):
    heads = all_ref.shape[0]
    gen, level, used = levels(group_ref, t_ref)
    for s in range(heads):
        keys_ref[64 * s : 64 * s + 64, 0:128] = all_ref[s, 144:208, :]
    keys_ref[:, 128:256] = jnp.ones((64 * heads, 128), BF16)
    left = left_half((64, 128))
    own = own_ref[144:208, :].astype(F32)
    stacked = jnp.concatenate([jnp.where(left, own, 0.0), jnp.where(left, 0.0, own)], axis=0)
    stacked = stacked.astype(BF16)
    const_sum = jnp.zeros((16, 128), F32)
    for h in range(heads):
        block = all_ref[h, 0:128, :]
        const = all_ref[h, 128:144, :].astype(F32)
        const_sum = const_sum + const
        query = dot(stacked, block)
        rows = slice(64 * h, 64 * h + 64)
        query_ref[0, rows, :] = jnp.where(left, query[0:64] + const[0:1], 0.0).astype(BF16)
        query_ref[1, rows, :] = jnp.where(left, 0.0, query[64:128] + const[1:2]).astype(BF16)
    step = 256
    wide_left = left_half((step, 128))
    for i in range(2):
        for at in range(0, 64 * heads, step):
            rows = slice(at, at + step)
            scores = dot(query_ref[i, rows, :], keys_ref[:, 0:128], 1, 1)
            top = jnp.max(scores, axis=1, keepdims=True)
            weights = jnp.exp2(scores - top).astype(BF16)
            mixed = dot(weights, keys_ref[...])
            mixed = mixed[:, 0:128] / mixed[:, 128:256]
            keep = wide_left if i == 0 else jnp.logical_not(wide_left)
            mixed_ref[i, rows, :] = jnp.where(keep, mixed, 0.0).astype(BF16)
    total = dot(stacked, local_ref[0:128, :].astype(BF16))
    for h in range(heads):
        rows = slice(64 * h, 64 * h + 64)
        pair = jnp.concatenate([mixed_ref[0, rows, :], mixed_ref[1, rows, :]], axis=0)
        total = total + dot(pair, all_ref[h, 0:128, :])
    first = used[0] * (total[0:64] + const_sum[0:1] + local_ref[128:129, :])
    second = used[1] * (total[64:128] + const_sum[1:2] + local_ref[128:129, :])
    moved = jnp.where(left, second, first)
    for g in range(moved_ref.shape[0]):
        moved_ref[g] = moved.astype(BF16)
    for i, part in ((0, moved[:, 64:128]), (1, moved[:, 0:64])):
        noisy = noisy_latent(level[i], prev_ref[i], noise_ref[i])
        prediction_ref[0, i] = gen * gen_ref[i].astype(F32) + (1.0 - gen) * noisy - part


def guidance(moved_ref):
    return 2.5 * moved_ref[1].astype(F32) - 1.5 * moved_ref[2].astype(F32)


def partial_kernel(group_ref, t_ref, moved_ref, noise_ref, prev_ref, saved_ref, out_ref):
    guided = guidance(moved_ref)
    down = moved_ref[3].astype(F32) - guided
    halves = (slice(64, 128), slice(0, 64))
    row = lax.broadcasted_iota(jnp.int32, (16, 128), 0)
    sums = []
    for i in range(2):
        level = (t_ref[i].astype(F32) + 0.5) * (1.0 / NOISE_LEVEL_COUNT)
        real = noisy_latent(level, prev_ref[i], noise_ref[i]) - guided[:, halves[i]]
        gap = jnp.abs(prev_ref[i] - real)
        sums.append(jnp.sum(jnp.sum(gap, axis=0, keepdims=True), axis=1, keepdims=True))
    sums = jnp.where(row < 8, sums[0], sums[1])
    high = sums.astype(BF16).astype(F32)
    sums = jnp.where(left_half((16, 128)), high, sums - high).astype(BF16)
    tokens = jnp.concatenate([down[:, halves[0]], down[:, halves[1]]], axis=0).astype(BF16)
    out_row = lax.broadcasted_iota(jnp.int32, (128, 64), 0)
    channel = lax.broadcasted_iota(jnp.int32, (128, 64), 1)
    pick = jnp.where((out_row // 16) * 8 + out_row % 8 == channel, 1.0, 0.0).astype(BF16)
    spread_out = dot(pick, tokens, 1, 1)
    image = (lax.broadcasted_iota(jnp.int32, (128, 128), 0) % 16) // 8
    owner = lax.broadcasted_iota(jnp.int32, (128, 128), 1) // 64
    spread_out = jnp.where(image == owner, spread_out, 0.0).astype(BF16)
    saved = jnp.concatenate([saved_ref[0], saved_ref[1]], axis=0)
    grad = dot(spread_out, saved).astype(BF16)
    for a in range(8):
        for b in range(2):
            out_ref[2 * a + b, :, 0:384] = grad[16 * a : 16 * a + 16, 384 * b : 384 * b + 384]
            out_ref[2 * a + b, :, 384:512] = sums


def scale_kernel(factor, part_ref, moved_ref, out_ref, grad_ref):
    total = part_ref[0].astype(F32)
    for s in range(1, part_ref.shape[0]):
        total = total + part_ref[s].astype(F32)
    spread = (total[:, 384:385] + total[:, 448:449]) * (1.0 / (NTOK * 64)) + 1e-05
    grad = total[:, 0:384] * (factor / spread)
    grad = grad[0:8] + grad[8:16]
    for k in range(out_ref.shape[0]):
        out_ref[k] = grad
    gap = guidance(moved_ref) - moved_ref[3].astype(F32)
    grad_ref[0] = gap[:, 64:128] / spread[0:1]
    grad_ref[1] = gap[:, 0:64] / spread[8:9]


def sum_kernel(copies, part_ref, out_ref):
    for g in range(part_ref.shape[0] // copies):
        total = part_ref[g * copies]
        for d in range(1, copies):
            total = total + part_ref[g * copies + d]
        out_ref[:, 384 * g : 384 * g + 384] = total


def place_kernel(part_ref, out_ref):
    for a in range(8):
        for b in range(2):
            for g in range(4):
                out_ref[8 * a : 8 * a + 8, 768 * g + 384 * b : 768 * g + 384 * b + 384] = part_ref[
                    2 * a + b, :, 384 * g : 384 * g + 384
                ]


SCALAR = pl.BlockSpec(memory_space=pltpu.SMEM)
VECTOR = pl.BlockSpec(memory_space=pltpu.VMEM)


def params(mib):
    return pltpu.CompilerParams(vmem_limit_bytes=mib << 20)


def shape_of(shape, dtype):
    return jax.ShapeDtypeStruct(shape, dtype)


def per_device(
    noise_gen,
    noise_score,
    prev_latents,
    t_idx,
    w_in,
    w_qkv,
    w_out,
    w_final,
    mod_scale,
    mod_shift,
    saved_features,
):
    groups = lax.axis_size("group")
    heads = lax.axis_size("seq")
    copies = lax.axis_size("dp")
    group = lax.axis_index("group").astype(jnp.int32).reshape(1)
    width = w_in.shape[2]

    sent, local = pl.pallas_call(
        fold_kernel,
        out_shape=(shape_of((ROWS, 128), BF16), shape_of((136, 128), F32)),
        in_specs=[SCALAR] * 2 + [VECTOR] * 9,
        out_specs=(VECTOR, VECTOR),
        scratch_shapes=[pltpu.VMEM((144, width), BF16)],
        compiler_params=params(24),
        name="fold",
    )(
        group, t_idx, noise_gen, noise_score, prev_latents, w_in,
        w_qkv[0].transpose(1, 0, 2), w_out[0].T, w_final[0].T, mod_scale, mod_shift,
    )
    everyone = lax.all_gather(sent, "seq", axis=0, tiled=True).reshape(heads, ROWS, 128)

    moved, prediction = pl.pallas_call(
        attend_kernel,
        out_shape=(shape_of((groups, 64, 128), BF16), shape_of((1, 2, 64, 64), F32)),
        in_specs=[SCALAR] * 2 + [VECTOR] * 6,
        out_specs=(VECTOR, VECTOR),
        scratch_shapes=[
            pltpu.VMEM((64 * heads, 256), BF16),
            pltpu.VMEM((2, 64 * heads, 128), BF16),
            pltpu.VMEM((2, 64 * heads, 128), BF16),
        ],
        compiler_params=params(32),
        name="attend",
    )(group, t_idx, noise_gen, noise_score, prev_latents, everyone, sent, local)
    moved = lax.all_to_all(moved, "group", 0, 0, tiled=True)

    quarter = width // groups
    whole = lambda *dims: pl.BlockSpec(dims, lambda n, g, t: (0,) * len(dims))
    parts = pl.pallas_call(
        partial_kernel,
        out_shape=shape_of((heads, 16, 512), BF16),
        grid_spec=pltpu.PrefetchScalarGridSpec(
            num_scalar_prefetch=2,
            grid=(1,),
            in_specs=[
                whole(groups, 64, 128),
                whole(2, 64, 64),
                whole(2, 64, 64),
                pl.BlockSpec((2, 64, quarter), lambda n, g, t: (0, 0, g[0])),
            ],
            out_specs=whole(heads, 16, 512),
        ),
        compiler_params=params(16),
        name="partial",
    )(group, t_idx, moved, noise_score, prev_latents, saved_features)
    parts = lax.all_to_all(parts, "seq", 0, 0, tiled=True)

    factor = 1.0 / math.sqrt(2 * copies * NTOK)
    summed, dmd_grad = pl.pallas_call(
        lambda *refs: scale_kernel(factor, *refs),
        out_shape=(shape_of((groups * copies, 8, 384), F32), shape_of((2, 64, 64), F32)),
        in_specs=[VECTOR] * 2,
        out_specs=(VECTOR, VECTOR),
        compiler_params=params(16),
        name="scale",
    )(parts, moved)
    summed = lax.all_to_all(summed, ("group", "dp"), 0, 0, tiled=True)

    rows = pl.pallas_call(
        lambda *refs: sum_kernel(copies, *refs),
        out_shape=shape_of((8, 384 * groups), F32),
        in_specs=[VECTOR],
        out_specs=VECTOR,
        compiler_params=params(16),
        name="sum",
    )(summed)
    rows = lax.all_gather(rows, "seq", axis=0, tiled=True).reshape(heads, 8, 384 * groups)

    total = pl.pallas_call(
        place_kernel,
        out_shape=shape_of((64, width), F32),
        in_specs=[VECTOR],
        out_specs=VECTOR,
        compiler_params=params(16),
        name="place",
    )(rows)
    return prediction, dmd_grad, total.T


def solution(mesh):
    placed = (
        P("dp", "seq", None),
        P("dp", "seq", None),
        P("dp", "seq", None),
        P("dp"),
        P("group", None, None),
        P("group", None, None, "seq"),
        P("group", "seq", None),
        P("group", None, None),
        P("group", None),
        P("group", None),
        P("dp", "seq", None),
    )
    return jax.shard_map(
        per_device,
        mesh=mesh,
        in_specs=placed,
        out_specs=(P("group", "dp", "seq", None), P("dp", "seq", None), P()),
        check_vma=False,
    )
```

```python
import math

import jax
import jax.numpy as jnp
from jax import lax
from jax.experimental import pallas as pl
from jax.experimental.pallas import tpu as pltpu
from jax.sharding import PartitionSpec as P

NTOK = 1024
NOISE_LEVEL_COUNT = 1000
BF16 = jnp.bfloat16
F32 = jnp.float32
ROWS = 208


def dot(a, b, lhs=1, rhs=0):
    return lax.dot_general(a, b, (((lhs,), (rhs,)), ((), ())), preferred_element_type=F32)


def left_half(shape):
    return lax.broadcasted_iota(jnp.int32, shape, 1) < 64


def levels(group_ref, t_ref):
    gen = jnp.where(group_ref[0] == 0, 1.0, 0.0).astype(F32)
    level = [(t_ref[i].astype(F32) + 0.5) * (1.0 / NOISE_LEVEL_COUNT) for i in range(2)]
    return gen, level, [gen + (1.0 - gen) * value for value in level]


def noisy_latent(level, prev, noise):
    return (1.0 - level) * prev + level * noise.astype(F32)


def fold_kernel(group_ref, t_ref, *refs):
    sources, (sent_ref, local_ref), held = refs[:9], refs[9:11], refs[11:20]
    left_ref, arrived = refs[20:]
    loads = [
        pltpu.make_async_copy(sources[k], held[k], arrived.at[k]) for k in range(len(sources))
    ]
    for load in loads:
        load.start()
    prev_ref, gen_ref, noise_ref, w_in_ref, scale_ref, shift_ref = held[:6]
    w_out_ref, w_final_ref, w_qkv_ref = held[6:]
    for load in loads[:6]:
        load.wait()
    width = w_in_ref.shape[2]
    gen, level, used = levels(group_ref, t_ref)
    latents = []
    for i in range(2):
        noisy = noisy_latent(level[i], prev_ref[i], noise_ref[i])
        latents.append(gen * gen_ref[i].astype(F32) + (1.0 - gen) * noisy)
    latent = jnp.concatenate(latents, axis=0).astype(BF16)
    step = 512
    squares = jnp.zeros((128, step), F32)
    for at in range(0, width, step):
        part = w_in_ref[0, :, at : at + step]
        projected = dot(latent, part)
        squares = squares + projected * projected
        scale = scale_ref[:, at : at + step]
        shift = shift_ref[:, at : at + step]
        high = shift.astype(BF16).astype(F32)
        row = lax.broadcasted_iota(jnp.int32, (16, step), 0)
        left_ref[0:64, at : at + step] = part
        left_ref[64:128, at : at + step] = (part.astype(F32) * scale).astype(BF16)
        left_ref[128:144, at : at + step] = jnp.where(
            row == 0, high, jnp.where(row == 1, shift - high, 0.0)
        ).astype(BF16)
    mean = jnp.sum(squares, axis=1, keepdims=True) * (1.0 / width)
    scaled = (latent.astype(F32) * lax.rsqrt(mean + 1e-06)).astype(BF16)
    sent_ref[144:208, :] = jnp.concatenate([scaled[0:64], scaled[64:128]], axis=1)

    for load in loads[6:]:
        load.wait()
    folded = [dot(left_ref[...], w_qkv_ref[c]) for c in range(3)]
    final = dot(left_ref[...], w_final_ref[...], 1, 1)
    const = [part[128:129] + part[129:130] for part in folded]
    final_const = final[128:129] + final[129:130]
    factor = math.log2(math.e) / math.sqrt(128.0)
    w_out = w_out_ref[...]
    blocks, consts, locals_ = [], [], []
    value_const = dot(jnp.broadcast_to(const[2], (16, 128)).astype(BF16), w_out, 1, 1)
    for i in range(2):
        q, k, v = [(part[0:64] + used[i] * part[64:128]) for part in folded]
        kb = k.astype(BF16)
        scores = dot(q.astype(BF16), kb, 1, 1) * factor
        out = dot(v.astype(BF16), w_out, 1, 1)
        key_const = dot(jnp.broadcast_to(const[0], (16, 128)).astype(BF16), kb, 1, 1) * factor
        local = final[0:64] + used[i] * final[64:128]
        zero = jnp.zeros_like(local)
        if i == 0:
            blocks.append(jnp.concatenate([scores, out], axis=1))
            consts.append(jnp.concatenate([key_const, value_const], axis=1))
            locals_.append(jnp.concatenate([zero, local], axis=1))
        else:
            blocks.append(jnp.concatenate([out, scores], axis=1))
            consts.append(jnp.concatenate([value_const, key_const], axis=1))
            locals_.append(jnp.concatenate([local, zero], axis=1))
    sent_ref[0:64, :] = blocks[0].astype(BF16)
    sent_ref[64:128, :] = blocks[1].astype(BF16)
    row = lax.broadcasted_iota(jnp.int32, (16, 128), 0)
    sent_ref[128:144, :] = jnp.where(row == 0, consts[0], consts[1]).astype(BF16)
    local_ref[0:64, :] = locals_[0]
    local_ref[64:128, :] = locals_[1]
    both = jnp.concatenate([final_const, final_const], axis=1)
    local_ref[128:136, :] = jnp.broadcast_to(both, (8, 128))


def attend_kernel(
    group_ref, t_ref, gen_ref, noise_ref, prev_ref, all_ref, own_ref, local_ref,
    moved_ref, prediction_ref, keys_ref, query_ref, mixed_ref,
):
    heads = all_ref.shape[0]
    gen, level, used = levels(group_ref, t_ref)
    for s in range(heads):
        keys_ref[64 * s : 64 * s + 64, 0:128] = all_ref[s, 144:208, :]
    keys_ref[:, 128:256] = jnp.ones((64 * heads, 128), BF16)
    left = left_half((64, 128))
    own = own_ref[144:208, :].astype(F32)
    stacked = jnp.concatenate([jnp.where(left, own, 0.0), jnp.where(left, 0.0, own)], axis=0)
    stacked = stacked.astype(BF16)
    const_sum = jnp.zeros((16, 128), F32)
    for h in range(heads):
        block = all_ref[h, 0:128, :]
        const = all_ref[h, 128:144, :].astype(F32)
        const_sum = const_sum + const
        query = dot(stacked, block)
        rows = slice(64 * h, 64 * h + 64)
        query_ref[0, rows, :] = jnp.where(left, query[0:64] + const[0:1], 0.0).astype(BF16)
        query_ref[1, rows, :] = jnp.where(left, 0.0, query[64:128] + const[1:2]).astype(BF16)
    step = 256
    wide_left = left_half((step, 128))
    for i in range(2):
        for at in range(0, 64 * heads, step):
            rows = slice(at, at + step)
            scores = dot(query_ref[i, rows, :], keys_ref[:, 0:128], 1, 1)
            top = jnp.max(scores, axis=1, keepdims=True)
            weights = jnp.exp2(scores - top).astype(BF16)
            mixed = dot(weights, keys_ref[...])
            mixed = mixed[:, 0:128] / mixed[:, 128:256]
            keep = wide_left if i == 0 else jnp.logical_not(wide_left)
            mixed_ref[i, rows, :] = jnp.where(keep, mixed, 0.0).astype(BF16)
    total = dot(stacked, local_ref[0:128, :].astype(BF16))
    for h in range(heads):
        rows = slice(64 * h, 64 * h + 64)
        pair = jnp.concatenate([mixed_ref[0, rows, :], mixed_ref[1, rows, :]], axis=0)
        total = total + dot(pair, all_ref[h, 0:128, :])
    first = used[0] * (total[0:64] + const_sum[0:1] + local_ref[128:129, :])
    second = used[1] * (total[64:128] + const_sum[1:2] + local_ref[128:129, :])
    moved = jnp.where(left, second, first)
    for g in range(moved_ref.shape[0]):
        moved_ref[g] = moved.astype(BF16)
    for i, part in ((0, moved[:, 64:128]), (1, moved[:, 0:64])):
        noisy = noisy_latent(level[i], prev_ref[i], noise_ref[i])
        prediction_ref[0, i] = gen * gen_ref[i].astype(F32) + (1.0 - gen) * noisy - part


def guidance(moved_ref):
    return 2.5 * moved_ref[1].astype(F32) - 1.5 * moved_ref[2].astype(F32)


def partial_kernel(group_ref, t_ref, moved_ref, noise_ref, prev_ref, saved_ref, out_ref):
    guided = guidance(moved_ref)
    down = moved_ref[3].astype(F32) - guided
    halves = (slice(64, 128), slice(0, 64))
    row = lax.broadcasted_iota(jnp.int32, (16, 128), 0)
    sums = []
    for i in range(2):
        level = (t_ref[i].astype(F32) + 0.5) * (1.0 / NOISE_LEVEL_COUNT)
        real = noisy_latent(level, prev_ref[i], noise_ref[i]) - guided[:, halves[i]]
        gap = jnp.abs(prev_ref[i] - real)
        sums.append(jnp.sum(jnp.sum(gap, axis=0, keepdims=True), axis=1, keepdims=True))
    sums = jnp.where(row < 8, sums[0], sums[1])
    high = sums.astype(BF16).astype(F32)
    sums = jnp.where(left_half((16, 128)), high, sums - high).astype(BF16)
    tokens = jnp.concatenate([down[:, halves[0]], down[:, halves[1]]], axis=0).astype(BF16)
    out_row = lax.broadcasted_iota(jnp.int32, (128, 64), 0)
    channel = lax.broadcasted_iota(jnp.int32, (128, 64), 1)
    pick = jnp.where((out_row // 16) * 8 + out_row % 8 == channel, 1.0, 0.0).astype(BF16)
    spread_out = dot(pick, tokens, 1, 1)
    image = (lax.broadcasted_iota(jnp.int32, (128, 128), 0) % 16) // 8
    owner = lax.broadcasted_iota(jnp.int32, (128, 128), 1) // 64
    spread_out = jnp.where(image == owner, spread_out, 0.0).astype(BF16)
    saved = jnp.concatenate([saved_ref[0], saved_ref[1]], axis=0)
    grad = dot(spread_out, saved).astype(BF16)
    for a in range(8):
        for b in range(2):
            out_ref[2 * a + b, :, 0:384] = grad[16 * a : 16 * a + 16, 384 * b : 384 * b + 384]
            out_ref[2 * a + b, :, 384:512] = sums


def scale_kernel(factor, part_ref, moved_ref, out_ref, grad_ref):
    total = part_ref[0].astype(F32)
    for s in range(1, part_ref.shape[0]):
        total = total + part_ref[s].astype(F32)
    spread = (total[:, 384:385] + total[:, 448:449]) * (1.0 / (NTOK * 64)) + 1e-05
    grad = total[:, 0:384] * (factor / spread)
    grad = grad[0:8] + grad[8:16]
    pair = jnp.concatenate([grad, grad], axis=0).astype(BF16)
    for at in range(0, out_ref.shape[0], 16):
        out_ref[at : at + 16, :] = pair
    gap = guidance(moved_ref) - moved_ref[3].astype(F32)
    grad_ref[0] = gap[:, 64:128] / spread[0:1]
    grad_ref[1] = gap[:, 0:64] / spread[8:9]


def sum_kernel(part_ref, out_ref):
    groups = out_ref.shape[1] // 384
    rows = part_ref.shape[0] // groups
    for g in range(groups):
        total = part_ref[g * rows : g * rows + 16, :].astype(F32)
        for at in range(g * rows + 16, (g + 1) * rows, 16):
            total = total + part_ref[at : at + 16, :].astype(F32)
        out_ref[:, 384 * g : 384 * g + 384] = total[0:8] + total[8:16]


def place_kernel(part_ref, out_ref):
    for a in range(8):
        for b in range(2):
            for g in range(4):
                out_ref[8 * a : 8 * a + 8, 768 * g + 384 * b : 768 * g + 384 * b + 384] = part_ref[
                    2 * a + b, :, 384 * g : 384 * g + 384
                ]


SCALAR = pl.BlockSpec(memory_space=pltpu.SMEM)
VECTOR = pl.BlockSpec(memory_space=pltpu.VMEM)


def params(mib):
    return pltpu.CompilerParams(vmem_limit_bytes=mib << 20)


def shape_of(shape, dtype):
    return jax.ShapeDtypeStruct(shape, dtype)


def per_device(
    noise_gen,
    noise_score,
    prev_latents,
    t_idx,
    w_in,
    w_qkv,
    w_out,
    w_final,
    mod_scale,
    mod_shift,
    saved_features,
):
    groups = lax.axis_size("group")
    heads = lax.axis_size("seq")
    copies = lax.axis_size("dp")
    group = lax.axis_index("group").astype(jnp.int32).reshape(1)
    width = w_in.shape[2]

    operands = (
        prev_latents, noise_gen, noise_score, w_in, mod_scale, mod_shift,
        w_out[0].T, w_final[0].T, w_qkv[0].transpose(1, 0, 2),
    )
    sent, local = pl.pallas_call(
        fold_kernel,
        out_shape=(shape_of((ROWS, 128), BF16), shape_of((136, 128), F32)),
        in_specs=[SCALAR] * 2 + [pl.BlockSpec(memory_space=pl.ANY)] * len(operands),
        out_specs=(VECTOR, VECTOR),
        scratch_shapes=[pltpu.VMEM(x.shape, x.dtype) for x in operands]
        + [pltpu.VMEM((144, width), BF16), pltpu.SemaphoreType.DMA((len(operands),))],
        compiler_params=params(58),
        name="fold",
    )(group, t_idx, *operands)
    everyone = lax.all_gather(sent, "seq", axis=0, tiled=True).reshape(heads, ROWS, 128)

    moved, prediction = pl.pallas_call(
        attend_kernel,
        out_shape=(shape_of((groups, 64, 128), BF16), shape_of((1, 2, 64, 64), F32)),
        in_specs=[SCALAR] * 2 + [VECTOR] * 6,
        out_specs=(VECTOR, VECTOR),
        scratch_shapes=[
            pltpu.VMEM((64 * heads, 256), BF16),
            pltpu.VMEM((2, 64 * heads, 128), BF16),
            pltpu.VMEM((2, 64 * heads, 128), BF16),
        ],
        compiler_params=params(32),
        name="attend",
    )(group, t_idx, noise_gen, noise_score, prev_latents, everyone, sent, local)
    moved = lax.all_to_all(moved, "group", 0, 0, tiled=True)

    quarter = width // groups
    whole = lambda *dims: pl.BlockSpec(dims, lambda n, g, t: (0,) * len(dims))
    parts = pl.pallas_call(
        partial_kernel,
        out_shape=shape_of((heads, 16, 512), BF16),
        grid_spec=pltpu.PrefetchScalarGridSpec(
            num_scalar_prefetch=2,
            grid=(1,),
            in_specs=[
                whole(groups, 64, 128),
                whole(2, 64, 64),
                whole(2, 64, 64),
                pl.BlockSpec((2, 64, quarter), lambda n, g, t: (0, 0, g[0])),
            ],
            out_specs=whole(heads, 16, 512),
        ),
        compiler_params=params(16),
        name="partial",
    )(group, t_idx, moved, noise_score, prev_latents, saved_features)
    parts = lax.all_to_all(parts, "seq", 0, 0, tiled=True)

    factor = 1.0 / math.sqrt(2 * copies * NTOK)
    summed, dmd_grad = pl.pallas_call(
        lambda *refs: scale_kernel(factor, *refs),
        out_shape=(shape_of((groups * copies * 8, 384), BF16), shape_of((2, 64, 64), F32)),
        in_specs=[VECTOR] * 2,
        out_specs=(VECTOR, VECTOR),
        compiler_params=params(16),
        name="scale",
    )(parts, moved)
    summed = lax.all_to_all(summed, ("group", "dp"), 0, 0, tiled=True)

    rows = pl.pallas_call(
        sum_kernel,
        out_shape=shape_of((8, 384 * groups), F32),
        in_specs=[VECTOR],
        out_specs=VECTOR,
        compiler_params=params(16),
        name="sum",
    )(summed)
    rows = lax.all_gather(rows, "seq", axis=0, tiled=True).reshape(heads, 8, 384 * groups)

    total = pl.pallas_call(
        place_kernel,
        out_shape=shape_of((64, width), F32),
        in_specs=[VECTOR],
        out_specs=VECTOR,
        compiler_params=params(16),
        name="place",
    )(rows)
    return prediction, dmd_grad, total.T


def solution(mesh):
    placed = (
        P("dp", "seq", None),
        P("dp", "seq", None),
        P("dp", "seq", None),
        P("dp"),
        P("group", None, None),
        P("group", None, None, "seq"),
        P("group", "seq", None),
        P("group", None, None),
        P("group", None),
        P("group", None),
        P("dp", "seq", None),
    )
    return jax.shard_map(
        per_device,
        mesh=mesh,
        in_specs=placed,
        out_specs=(P("group", "dp", "seq", None), P("dp", "seq", None), P()),
        check_vma=False,
    )
```

```python
import math

import jax
import jax.numpy as jnp
from jax import lax
from jax.experimental import pallas as pl
from jax.experimental.pallas import tpu as pltpu
from jax.sharding import PartitionSpec as P

NTOK = 1024
NOISE_LEVEL_COUNT = 1000
BF16 = jnp.bfloat16
F32 = jnp.float32
CHUNKS = 3
ROWS = 208


def dot(a, b, lhs=1, rhs=0):
    return lax.dot_general(a, b, (((lhs,), (rhs,)), ((), ())), preferred_element_type=F32)


def left_half(shape):
    return lax.broadcasted_iota(jnp.int32, shape, 1) < 64


def levels(group_ref, t_ref):
    gen = jnp.where(group_ref[0] == 0, 1.0, 0.0).astype(F32)
    level = [(t_ref[i].astype(F32) + 0.5) * (1.0 / NOISE_LEVEL_COUNT) for i in range(2)]
    return gen, level, [gen + (1.0 - gen) * value for value in level]


def noisy_latent(level, prev, noise):
    return (1.0 - level) * prev + level * noise.astype(F32)


def fold_kernel(group_ref, t_ref, *refs):
    sources, (sent_ref, local_ref), held = refs[:9], refs[9:11], refs[11:20]
    left_ref, arrived = refs[20:]
    width = sources[3].shape[2]
    step = width // CHUNKS
    pairs = [(sources[k], held[k]) for k in (0, 1, 2, 4, 5, 6)]
    for at in range(0, width, step):
        part = pl.ds(at, step)
        pairs.append((sources[3].at[:, :, part], held[3].at[:, :, part]))
        pairs.append((sources[7].at[:, part], held[7].at[:, part]))
        pairs += [(sources[8].at[c, part], held[8].at[c, part]) for c in range(3)]
    loads = [pltpu.make_async_copy(*pair, arrived.at[k]) for k, pair in enumerate(pairs)]
    for load in loads:
        load.start()
    prev_ref, gen_ref, noise_ref, w_in_ref, scale_ref, shift_ref = held[:6]
    w_out_ref, w_final_ref, w_qkv_ref = held[6:]
    for load in loads[:6]:
        load.wait()
    gen, level, used = levels(group_ref, t_ref)
    latents = []
    for i in range(2):
        noisy = noisy_latent(level[i], prev_ref[i], noise_ref[i])
        latents.append(gen * gen_ref[i].astype(F32) + (1.0 - gen) * noisy)
    latent = jnp.concatenate(latents, axis=0).astype(BF16)
    squares = jnp.zeros((128, 128), F32)
    final = jnp.zeros((144, 64), F32)
    folded = [jnp.zeros((144, 128), F32) for _ in range(3)]
    row = lax.broadcasted_iota(jnp.int32, (16, step), 0)
    for n in range(CHUNKS):
        at = n * step
        for load in loads[6 + 5 * n : 11 + 5 * n]:
            load.wait()
        part = w_in_ref[0, :, at : at + step]
        projected = dot(latent, part)
        for lane in range(0, step, 128):
            piece = projected[:, lane : lane + 128]
            squares = squares + piece * piece
        shift = shift_ref[:, at : at + step]
        high = shift.astype(BF16).astype(F32)
        shifts = jnp.where(row == 0, high, jnp.where(row == 1, shift - high, 0.0))
        scaled = part.astype(F32) * scale_ref[:, at : at + step]
        left_ref[0:64, :] = part
        left_ref[64:128, :] = scaled.astype(BF16)
        left_ref[128:144, :] = shifts.astype(BF16)
        final = final + dot(left_ref[...], w_final_ref[:, at : at + step], 1, 1)
        for c in range(3):
            folded[c] = folded[c] + dot(left_ref[...], w_qkv_ref[c, at : at + step, :])
    mean = jnp.sum(squares, axis=1, keepdims=True) * (1.0 / width)
    scaled = (latent.astype(F32) * lax.rsqrt(mean + 1e-06)).astype(BF16)
    sent_ref[144:208, :] = jnp.concatenate([scaled[0:64], scaled[64:128]], axis=1)
    const = [part[128:129] + part[129:130] for part in folded]
    final_const = final[128:129] + final[129:130]
    factor = math.log2(math.e) / math.sqrt(128.0)
    w_out = w_out_ref[...]
    blocks, consts, locals_ = [], [], []
    value_const = dot(jnp.broadcast_to(const[2], (16, 128)).astype(BF16), w_out, 1, 1)
    for i in range(2):
        q, k, v = [(part[0:64] + used[i] * part[64:128]) for part in folded]
        kb = k.astype(BF16)
        scores = dot(q.astype(BF16), kb, 1, 1) * factor
        out = dot(v.astype(BF16), w_out, 1, 1)
        key_const = dot(jnp.broadcast_to(const[0], (16, 128)).astype(BF16), kb, 1, 1) * factor
        local = final[0:64] + used[i] * final[64:128]
        zero = jnp.zeros_like(local)
        if i == 0:
            blocks.append(jnp.concatenate([scores, out], axis=1))
            consts.append(jnp.concatenate([key_const, value_const], axis=1))
            locals_.append(jnp.concatenate([zero, local], axis=1))
        else:
            blocks.append(jnp.concatenate([out, scores], axis=1))
            consts.append(jnp.concatenate([value_const, key_const], axis=1))
            locals_.append(jnp.concatenate([local, zero], axis=1))
    sent_ref[0:64, :] = blocks[0].astype(BF16)
    sent_ref[64:128, :] = blocks[1].astype(BF16)
    row = lax.broadcasted_iota(jnp.int32, (16, 128), 0)
    sent_ref[128:144, :] = jnp.where(row == 0, consts[0], consts[1]).astype(BF16)
    local_ref[0:64, :] = locals_[0]
    local_ref[64:128, :] = locals_[1]
    both = jnp.concatenate([final_const, final_const], axis=1)
    local_ref[128:136, :] = jnp.broadcast_to(both, (8, 128))


def attend_kernel(
    group_ref, me_ref, t_ref, gen_ref, noise_ref, prev_ref, all_ref, local_source,
    moved_ref, prediction_ref, keys_ref, query_ref, mixed_ref, local_ref, arrived,
):
    load = pltpu.make_async_copy(local_source, local_ref, arrived)
    load.start()
    heads = all_ref.shape[0]
    gen, level, used = levels(group_ref, t_ref)
    for s in range(heads):
        keys_ref[64 * s : 64 * s + 64, 0:128] = all_ref[s, 144:208, :]
    keys_ref[:, 128:256] = jnp.ones((64 * heads, 128), BF16)
    left = left_half((64, 128))
    own = all_ref[me_ref[0], 144:208, :].astype(F32)
    stacked = jnp.concatenate([jnp.where(left, own, 0.0), jnp.where(left, 0.0, own)], axis=0)
    stacked = stacked.astype(BF16)
    const_sum = jnp.zeros((16, 128), F32)
    for h in range(heads):
        block = all_ref[h, 0:128, :]
        const = all_ref[h, 128:144, :].astype(F32)
        const_sum = const_sum + const
        query = dot(stacked, block)
        rows = slice(64 * h, 64 * h + 64)
        query_ref[0, rows, :] = jnp.where(left, query[0:64] + const[0:1], 0.0).astype(BF16)
        query_ref[1, rows, :] = jnp.where(left, 0.0, query[64:128] + const[1:2]).astype(BF16)
    step = 256
    wide_left = left_half((step, 128))
    for i in range(2):
        for at in range(0, 64 * heads, step):
            rows = slice(at, at + step)
            scores = dot(query_ref[i, rows, :], keys_ref[:, 0:128], 1, 1)
            top = jnp.max(scores, axis=1, keepdims=True)
            weights = jnp.exp2(scores - top).astype(BF16)
            mixed = dot(weights, keys_ref[...])
            mixed = mixed[:, 0:128] / mixed[:, 128:256]
            keep = wide_left if i == 0 else jnp.logical_not(wide_left)
            mixed_ref[i, rows, :] = jnp.where(keep, mixed, 0.0).astype(BF16)
    load.wait()
    total = dot(stacked, local_ref[0:128, :].astype(BF16))
    for h in range(heads):
        rows = slice(64 * h, 64 * h + 64)
        pair = jnp.concatenate([mixed_ref[0, rows, :], mixed_ref[1, rows, :]], axis=0)
        total = total + dot(pair, all_ref[h, 0:128, :])
    first = used[0] * (total[0:64] + const_sum[0:1] + local_ref[128:129, :])
    second = used[1] * (total[64:128] + const_sum[1:2] + local_ref[128:129, :])
    moved = jnp.where(left, second, first)
    for g in range(moved_ref.shape[0]):
        moved_ref[g] = moved.astype(BF16)
    for i, part in ((0, moved[:, 64:128]), (1, moved[:, 0:64])):
        noisy = noisy_latent(level[i], prev_ref[i], noise_ref[i])
        prediction_ref[0, i] = gen * gen_ref[i].astype(F32) + (1.0 - gen) * noisy - part


def guidance(moved_ref):
    return 2.5 * moved_ref[1].astype(F32) - 1.5 * moved_ref[2].astype(F32)


def partial_kernel(group_ref, t_ref, moved_ref, noise_ref, prev_ref, saved_ref, out_ref):
    guided = guidance(moved_ref)
    down = moved_ref[3].astype(F32) - guided
    halves = (slice(64, 128), slice(0, 64))
    row = lax.broadcasted_iota(jnp.int32, (16, 128), 0)
    sums = []
    for i in range(2):
        level = (t_ref[i].astype(F32) + 0.5) * (1.0 / NOISE_LEVEL_COUNT)
        real = noisy_latent(level, prev_ref[i], noise_ref[i]) - guided[:, halves[i]]
        gap = jnp.abs(prev_ref[i] - real)
        sums.append(jnp.sum(jnp.sum(gap, axis=0, keepdims=True), axis=1, keepdims=True))
    sums = jnp.where(row < 8, sums[0], sums[1])
    high = sums.astype(BF16).astype(F32)
    sums = jnp.where(left_half((16, 128)), high, sums - high).astype(BF16)
    tokens = jnp.concatenate([down[:, halves[0]], down[:, halves[1]]], axis=0).astype(BF16)
    out_row = lax.broadcasted_iota(jnp.int32, (128, 64), 0)
    channel = lax.broadcasted_iota(jnp.int32, (128, 64), 1)
    pick = jnp.where((out_row // 16) * 8 + out_row % 8 == channel, 1.0, 0.0).astype(BF16)
    spread_out = dot(pick, tokens, 1, 1)
    image = (lax.broadcasted_iota(jnp.int32, (128, 128), 0) % 16) // 8
    owner = lax.broadcasted_iota(jnp.int32, (128, 128), 1) // 64
    spread_out = jnp.where(image == owner, spread_out, 0.0).astype(BF16)
    saved = jnp.concatenate([saved_ref[0], saved_ref[1]], axis=0)
    grad = dot(spread_out, saved).astype(BF16)
    for a in range(8):
        for b in range(2):
            out_ref[2 * a + b, :, 0:384] = grad[16 * a : 16 * a + 16, 384 * b : 384 * b + 384]
            out_ref[2 * a + b, :, 384:512] = sums


def scale_kernel(factor, part_ref, moved_ref, out_ref, grad_ref):
    total = part_ref[0].astype(F32)
    for s in range(1, part_ref.shape[0]):
        total = total + part_ref[s].astype(F32)
    spread = (total[:, 384:385] + total[:, 448:449]) * (1.0 / (NTOK * 64)) + 1e-05
    grad = total[:, 0:384] * (factor / spread)
    grad = grad[0:8] + grad[8:16]
    pair = jnp.concatenate([grad, grad], axis=0).astype(BF16)
    for at in range(0, out_ref.shape[0], 16):
        out_ref[at : at + 16, :] = pair
    gap = guidance(moved_ref) - moved_ref[3].astype(F32)
    grad_ref[0] = gap[:, 64:128] / spread[0:1]
    grad_ref[1] = gap[:, 0:64] / spread[8:9]


def sum_kernel(part_ref, out_ref):
    groups = out_ref.shape[1] // 384
    rows = part_ref.shape[0] // groups
    for g in range(groups):
        total = part_ref[g * rows : g * rows + 16, :].astype(F32)
        for at in range(g * rows + 16, (g + 1) * rows, 16):
            total = total + part_ref[at : at + 16, :].astype(F32)
        out_ref[:, 384 * g : 384 * g + 384] = total[0:8] + total[8:16]


def place_kernel(part_ref, out_ref):
    for a in range(8):
        for b in range(2):
            for g in range(4):
                out_ref[8 * a : 8 * a + 8, 768 * g + 384 * b : 768 * g + 384 * b + 384] = part_ref[
                    2 * a + b, :, 384 * g : 384 * g + 384
                ]


SCALAR = pl.BlockSpec(memory_space=pltpu.SMEM)
VECTOR = pl.BlockSpec(memory_space=pltpu.VMEM)


def params(mib):
    return pltpu.CompilerParams(vmem_limit_bytes=mib << 20)


def shape_of(shape, dtype):
    return jax.ShapeDtypeStruct(shape, dtype)


def fold(group, t_idx, *operands):
    width = operands[3].shape[2]
    return pl.pallas_call(
        fold_kernel,
        out_shape=(shape_of((ROWS, 128), BF16), pltpu.VMEM((136, 128), F32)),
        in_specs=[SCALAR] * 2 + [pl.BlockSpec(memory_space=pl.ANY)] * len(operands),
        out_specs=(VECTOR, VECTOR),
        scratch_shapes=[pltpu.VMEM(x.shape, x.dtype) for x in operands]
        + [pltpu.VMEM((144, width // CHUNKS), BF16), pltpu.SemaphoreType.DMA((6 + 5 * CHUNKS,))],
        compiler_params=params(58),
        name="fold",
    )(group, t_idx, *operands)


def attend(groups, group, me, t_idx, noise_gen, noise_score, prev_latents, everyone, local):
    heads = everyone.shape[0]
    return pl.pallas_call(
        attend_kernel,
        out_shape=(shape_of((groups, 64, 128), BF16), shape_of((1, 2, 64, 64), F32)),
        in_specs=[SCALAR] * 3 + [VECTOR] * 4 + [pl.BlockSpec(memory_space=pl.ANY)],
        out_specs=(VECTOR, VECTOR),
        scratch_shapes=[
            pltpu.VMEM((64 * heads, 256), BF16),
            pltpu.VMEM((2, 64 * heads, 128), BF16),
            pltpu.VMEM((2, 64 * heads, 128), BF16),
            pltpu.VMEM(local.shape, F32),
            pltpu.SemaphoreType.DMA,
        ],
        compiler_params=params(32),
        name="attend",
    )(group, me, t_idx, noise_gen, noise_score, prev_latents, everyone, local)


def per_device(
    noise_gen,
    noise_score,
    prev_latents,
    t_idx,
    w_in,
    w_qkv,
    w_out,
    w_final,
    mod_scale,
    mod_shift,
    saved_features,
):
    groups = lax.axis_size("group")
    heads = lax.axis_size("seq")
    copies = lax.axis_size("dp")
    group = lax.axis_index("group").astype(jnp.int32).reshape(1)
    width = w_in.shape[2]

    operands = (
        prev_latents, noise_gen, noise_score, w_in, mod_scale, mod_shift,
        w_out[0].T, w_final[0].T, w_qkv[0].transpose(1, 0, 2),
    )
    sent, local = fold(group, t_idx, *operands)
    everyone = lax.all_gather(sent, "seq", axis=0, tiled=True).reshape(heads, ROWS, 128)

    me = lax.axis_index("seq").astype(jnp.int32).reshape(1)
    moved, prediction = attend(
        groups, group, me, t_idx, noise_gen, noise_score, prev_latents, everyone, local
    )
    moved = lax.all_to_all(moved, "group", 0, 0, tiled=True)

    quarter = width // groups
    whole = lambda *dims: pl.BlockSpec(dims, lambda n, g, t: (0,) * len(dims))
    parts = pl.pallas_call(
        partial_kernel,
        out_shape=shape_of((heads, 16, 512), BF16),
        grid_spec=pltpu.PrefetchScalarGridSpec(
            num_scalar_prefetch=2,
            grid=(1,),
            in_specs=[
                whole(groups, 64, 128),
                whole(2, 64, 64),
                whole(2, 64, 64),
                pl.BlockSpec((2, 64, quarter), lambda n, g, t: (0, 0, g[0])),
            ],
            out_specs=whole(heads, 16, 512),
        ),
        compiler_params=params(16),
        name="partial",
    )(group, t_idx, moved, noise_score, prev_latents, saved_features)
    parts = lax.all_to_all(parts, "seq", 0, 0, tiled=True)

    factor = 1.0 / math.sqrt(2 * copies * NTOK)
    summed, dmd_grad = pl.pallas_call(
        lambda *refs: scale_kernel(factor, *refs),
        out_shape=(shape_of((groups * copies * 8, 384), BF16), shape_of((2, 64, 64), F32)),
        in_specs=[VECTOR] * 2,
        out_specs=(VECTOR, VECTOR),
        compiler_params=params(16),
        name="scale",
    )(parts, moved)
    summed = lax.all_to_all(summed, ("group", "dp"), 0, 0, tiled=True)

    rows = pl.pallas_call(
        sum_kernel,
        out_shape=shape_of((8, 384 * groups), F32),
        in_specs=[VECTOR],
        out_specs=VECTOR,
        compiler_params=params(16),
        name="sum",
    )(summed)
    rows = lax.all_gather(rows, "seq", axis=0, tiled=True).reshape(heads, 8, 384 * groups)

    total = pl.pallas_call(
        place_kernel,
        out_shape=shape_of((64, width), F32),
        in_specs=[VECTOR],
        out_specs=VECTOR,
        compiler_params=params(16),
        name="place",
    )(rows)
    return prediction, dmd_grad, total.T


def solution(mesh):
    placed = (
        P("dp", "seq", None),
        P("dp", "seq", None),
        P("dp", "seq", None),
        P("dp"),
        P("group", None, None),
        P("group", None, None, "seq"),
        P("group", "seq", None),
        P("group", None, None),
        P("group", None),
        P("group", None),
        P("dp", "seq", None),
    )
    return jax.shard_map(
        per_device,
        mesh=mesh,
        in_specs=placed,
        out_specs=(P("group", "dp", "seq", None), P("dp", "seq", None), P()),
        check_vma=False,
    )
```

```python
import math

import jax
import jax.numpy as jnp
from jax import lax
from jax.experimental import pallas as pl
from jax.experimental.pallas import tpu as pltpu
from jax.sharding import PartitionSpec as P

NTOK = 1024
NOISE_LEVEL_COUNT = 1000
BF16 = jnp.bfloat16
F32 = jnp.float32
CHUNKS = 3
ROWS = 208


def dot(a, b, lhs=1, rhs=0):
    return lax.dot_general(a, b, (((lhs,), (rhs,)), ((), ())), preferred_element_type=F32)


def left_half(shape):
    return lax.broadcasted_iota(jnp.int32, shape, 1) < 64


def levels(group_ref, t_ref):
    gen = jnp.where(group_ref[0] == 0, 1.0, 0.0).astype(F32)
    level = [(t_ref[i].astype(F32) + 0.5) * (1.0 / NOISE_LEVEL_COUNT) for i in range(2)]
    return gen, level, [gen + (1.0 - gen) * value for value in level]


def noisy_latent(level, prev, noise):
    return (1.0 - level) * prev + level * noise.astype(F32)


def fold_kernel(group_ref, t_ref, *refs):
    sources, (sent_ref, local_ref), held = refs[:9], refs[9:11], refs[11:20]
    left_ref, arrived = refs[20:]
    width = sources[3].shape[2]
    step = width // CHUNKS
    pairs = [(sources[k], held[k]) for k in (0, 1, 2, 4, 5, 6)]
    for at in range(0, width, step):
        part = pl.ds(at, step)
        pairs.append((sources[3].at[:, :, part], held[3].at[:, :, part]))
        pairs.append((sources[7].at[:, part], held[7].at[:, part]))
        pairs += [(sources[8].at[c, part], held[8].at[c, part]) for c in range(3)]
    loads = [pltpu.make_async_copy(*pair, arrived.at[k]) for k, pair in enumerate(pairs)]
    for load in loads:
        load.start()
    prev_ref, gen_ref, noise_ref, w_in_ref, scale_ref, shift_ref = held[:6]
    w_out_ref, w_final_ref, w_qkv_ref = held[6:]
    for load in loads[:6]:
        load.wait()
    gen, level, used = levels(group_ref, t_ref)
    latents = []
    for i in range(2):
        noisy = noisy_latent(level[i], prev_ref[i], noise_ref[i])
        latents.append(gen * gen_ref[i].astype(F32) + (1.0 - gen) * noisy)
    latent = jnp.concatenate(latents, axis=0).astype(BF16)
    squares = jnp.zeros((128, 128), F32)
    final = jnp.zeros((144, 64), F32)
    folded = [jnp.zeros((144, 128), F32) for _ in range(3)]
    row = lax.broadcasted_iota(jnp.int32, (16, step), 0)
    for n in range(CHUNKS):
        at = n * step
        for load in loads[6 + 5 * n : 11 + 5 * n]:
            load.wait()
        part = w_in_ref[0, :, at : at + step]
        projected = dot(latent, part)
        for lane in range(0, step, 128):
            piece = projected[:, lane : lane + 128]
            squares = squares + piece * piece
        shift = shift_ref[:, at : at + step]
        high = shift.astype(BF16).astype(F32)
        shifts = jnp.where(row == 0, high, jnp.where(row == 1, shift - high, 0.0))
        scaled = part.astype(F32) * scale_ref[:, at : at + step]
        left_ref[0:64, :] = part
        left_ref[64:128, :] = scaled.astype(BF16)
        left_ref[128:144, :] = shifts.astype(BF16)
        final = final + dot(left_ref[...], w_final_ref[:, at : at + step], 1, 1)
        for c in range(3):
            folded[c] = folded[c] + dot(left_ref[...], w_qkv_ref[c, at : at + step, :])
    mean = jnp.sum(squares, axis=1, keepdims=True) * (1.0 / width)
    scaled = (latent.astype(F32) * lax.rsqrt(mean + 1e-06)).astype(BF16)
    sent_ref[144:208, :] = jnp.concatenate([scaled[0:64], scaled[64:128]], axis=1)
    const = [part[128:129] + part[129:130] for part in folded]
    final_const = final[128:129] + final[129:130]
    factor = math.log2(math.e) / math.sqrt(128.0)
    w_out = w_out_ref[...]
    blocks, consts, locals_ = [], [], []
    value_const = dot(jnp.broadcast_to(const[2], (16, 128)).astype(BF16), w_out, 1, 1)
    for i in range(2):
        q, k, v = [(part[0:64] + used[i] * part[64:128]) for part in folded]
        kb = k.astype(BF16)
        scores = dot(q.astype(BF16), kb, 1, 1) * factor
        out = dot(v.astype(BF16), w_out, 1, 1)
        key_const = dot(jnp.broadcast_to(const[0], (16, 128)).astype(BF16), kb, 1, 1) * factor
        local = final[0:64] + used[i] * final[64:128]
        zero = jnp.zeros_like(local)
        if i == 0:
            blocks.append(jnp.concatenate([scores, out], axis=1))
            consts.append(jnp.concatenate([key_const, value_const], axis=1))
            locals_.append(jnp.concatenate([zero, local], axis=1))
        else:
            blocks.append(jnp.concatenate([out, scores], axis=1))
            consts.append(jnp.concatenate([value_const, key_const], axis=1))
            locals_.append(jnp.concatenate([local, zero], axis=1))
    sent_ref[0:64, :] = blocks[0].astype(BF16)
    sent_ref[64:128, :] = blocks[1].astype(BF16)
    row = lax.broadcasted_iota(jnp.int32, (16, 128), 0)
    sent_ref[128:144, :] = jnp.where(row == 0, consts[0], consts[1]).astype(BF16)
    local_ref[0:64, :] = locals_[0]
    local_ref[64:128, :] = locals_[1]
    both = jnp.concatenate([final_const, final_const], axis=1)
    local_ref[128:136, :] = jnp.broadcast_to(both, (8, 128))


def attend_kernel(
    group_ref, me_ref, t_ref, gen_ref, noise_ref, prev_ref, all_ref, local_source,
    moved_ref, prediction_ref, keys_ref, query_ref, mixed_ref, local_ref, arrived,
):
    load = pltpu.make_async_copy(local_source, local_ref, arrived)
    load.start()
    heads = all_ref.shape[0]
    gen, level, used = levels(group_ref, t_ref)
    for s in range(heads):
        keys_ref[64 * s : 64 * s + 64, 0:128] = all_ref[s, 144:208, :]
    keys_ref[:, 128:256] = jnp.ones((64 * heads, 128), BF16)
    left = left_half((64, 128))
    own = all_ref[me_ref[0], 144:208, :].astype(F32)
    stacked = jnp.concatenate([jnp.where(left, own, 0.0), jnp.where(left, 0.0, own)], axis=0)
    stacked = stacked.astype(BF16)
    const_sum = jnp.zeros((16, 128), F32)
    for h in range(heads):
        block = all_ref[h, 0:128, :]
        const = all_ref[h, 128:144, :].astype(F32)
        const_sum = const_sum + const
        query = dot(stacked, block)
        rows = slice(64 * h, 64 * h + 64)
        query_ref[0, rows, :] = jnp.where(left, query[0:64] + const[0:1], 0.0).astype(BF16)
        query_ref[1, rows, :] = jnp.where(left, 0.0, query[64:128] + const[1:2]).astype(BF16)
    step = 256
    wide_left = left_half((step, 128))
    for i in range(2):
        for at in range(0, 64 * heads, step):
            rows = slice(at, at + step)
            scores = dot(query_ref[i, rows, :], keys_ref[:, 0:128], 1, 1)
            top = jnp.max(scores, axis=1, keepdims=True)
            weights = jnp.exp2(scores - top).astype(BF16)
            mixed = dot(weights, keys_ref[...])
            mixed = mixed[:, 0:128] / mixed[:, 128:256]
            keep = wide_left if i == 0 else jnp.logical_not(wide_left)
            mixed_ref[i, rows, :] = jnp.where(keep, mixed, 0.0).astype(BF16)
    load.wait()
    total = dot(stacked, local_ref[0:128, :].astype(BF16))
    for h in range(heads):
        rows = slice(64 * h, 64 * h + 64)
        pair = jnp.concatenate([mixed_ref[0, rows, :], mixed_ref[1, rows, :]], axis=0)
        total = total + dot(pair, all_ref[h, 0:128, :])
    first = used[0] * (total[0:64] + const_sum[0:1] + local_ref[128:129, :])
    second = used[1] * (total[64:128] + const_sum[1:2] + local_ref[128:129, :])
    moved = jnp.where(left, second, first)
    for g in range(moved_ref.shape[0]):
        moved_ref[g] = moved.astype(BF16)
    for i, part in ((0, moved[:, 64:128]), (1, moved[:, 0:64])):
        noisy = noisy_latent(level[i], prev_ref[i], noise_ref[i])
        prediction_ref[0, i] = gen * gen_ref[i].astype(F32) + (1.0 - gen) * noisy - part


def guidance(moved_ref):
    return 2.5 * moved_ref[1].astype(F32) - 1.5 * moved_ref[2].astype(F32)


def partial_kernel(group_ref, t_ref, moved_ref, noise_ref, prev_ref, saved_ref, out_ref):
    guided = guidance(moved_ref)
    down = moved_ref[3].astype(F32) - guided
    halves = (slice(64, 128), slice(0, 64))
    row = lax.broadcasted_iota(jnp.int32, (16, 128), 0)
    sums = []
    for i in range(2):
        level = (t_ref[i].astype(F32) + 0.5) * (1.0 / NOISE_LEVEL_COUNT)
        real = noisy_latent(level, prev_ref[i], noise_ref[i]) - guided[:, halves[i]]
        gap = jnp.abs(prev_ref[i] - real)
        sums.append(jnp.sum(jnp.sum(gap, axis=0, keepdims=True), axis=1, keepdims=True))
    sums = jnp.where(row < 8, sums[0], sums[1])
    high = sums.astype(BF16).astype(F32)
    sums = jnp.where(left_half((16, 128)), high, sums - high).astype(BF16)
    tokens = jnp.concatenate([down[:, halves[0]], down[:, halves[1]]], axis=0).astype(BF16)
    out_row = lax.broadcasted_iota(jnp.int32, (128, 64), 0)
    channel = lax.broadcasted_iota(jnp.int32, (128, 64), 1)
    pick = jnp.where((out_row // 16) * 8 + out_row % 8 == channel, 1.0, 0.0).astype(BF16)
    spread_out = dot(pick, tokens, 1, 1)
    image = (lax.broadcasted_iota(jnp.int32, (128, 128), 0) % 16) // 8
    owner = lax.broadcasted_iota(jnp.int32, (128, 128), 1) // 64
    spread_out = jnp.where(image == owner, spread_out, 0.0).astype(BF16)
    saved = jnp.concatenate([saved_ref[0], saved_ref[1]], axis=0)
    grad = dot(spread_out, saved).astype(BF16)
    for a in range(8):
        for b in range(2):
            out_ref[2 * a + b, :, 0:384] = grad[16 * a : 16 * a + 16, 384 * b : 384 * b + 384]
            out_ref[2 * a + b, :, 384:512] = sums


def scale_kernel(factor, part_ref, moved_ref, out_ref, grad_ref):
    total = part_ref[0].astype(F32)
    for s in range(1, part_ref.shape[0]):
        total = total + part_ref[s].astype(F32)
    spread = (total[:, 384:385] + total[:, 448:449]) * (1.0 / (NTOK * 64)) + 1e-05
    grad = total[:, 0:384] * (factor / spread)
    grad = grad[0:8] + grad[8:16]
    pair = jnp.concatenate([grad, grad], axis=0).astype(BF16)
    for at in range(0, out_ref.shape[0], 16):
        out_ref[at : at + 16, :] = pair
    gap = guidance(moved_ref) - moved_ref[3].astype(F32)
    grad_ref[0] = gap[:, 64:128] / spread[0:1]
    grad_ref[1] = gap[:, 0:64] / spread[8:9]


def sum_kernel(part_ref, out_ref):
    total = part_ref[0:16, :].astype(F32)
    for at in range(16, part_ref.shape[0], 16):
        total = total + part_ref[at : at + 16, :].astype(F32)
    total = total[0:8] + total[8:16]
    pair = jnp.concatenate([total, total], axis=0).astype(BF16)
    for at in range(0, out_ref.shape[0], 16):
        out_ref[at : at + 16, :] = pair


def place_kernel(part_ref, out_ref):
    at = 0
    for core in range(2):
        for g in range(4):
            lanes = slice(768 * g + 384 * core, 768 * g + 384 * core + 384)
            for row in range(0, 64, 16):
                out_ref[row : row + 16, lanes] = part_ref[at : at + 16, :].astype(F32)
                at += 16


SCALAR = pl.BlockSpec(memory_space=pltpu.SMEM)
VECTOR = pl.BlockSpec(memory_space=pltpu.VMEM)


def params(mib):
    return pltpu.CompilerParams(vmem_limit_bytes=mib << 20)


def shape_of(shape, dtype):
    return jax.ShapeDtypeStruct(shape, dtype)


def fold(group, t_idx, *operands):
    width = operands[3].shape[2]
    return pl.pallas_call(
        fold_kernel,
        out_shape=(shape_of((ROWS, 128), BF16), pltpu.VMEM((136, 128), F32)),
        in_specs=[SCALAR] * 2 + [pl.BlockSpec(memory_space=pl.ANY)] * len(operands),
        out_specs=(VECTOR, VECTOR),
        scratch_shapes=[pltpu.VMEM(x.shape, x.dtype) for x in operands]
        + [pltpu.VMEM((144, width // CHUNKS), BF16), pltpu.SemaphoreType.DMA((6 + 5 * CHUNKS,))],
        compiler_params=params(58),
        name="fold",
    )(group, t_idx, *operands)


def attend(groups, group, me, t_idx, noise_gen, noise_score, prev_latents, everyone, local):
    heads = everyone.shape[0]
    return pl.pallas_call(
        attend_kernel,
        out_shape=(shape_of((groups, 64, 128), BF16), shape_of((1, 2, 64, 64), F32)),
        in_specs=[SCALAR] * 3 + [VECTOR] * 4 + [pl.BlockSpec(memory_space=pl.ANY)],
        out_specs=(VECTOR, VECTOR),
        scratch_shapes=[
            pltpu.VMEM((64 * heads, 256), BF16),
            pltpu.VMEM((2, 64 * heads, 128), BF16),
            pltpu.VMEM((2, 64 * heads, 128), BF16),
            pltpu.VMEM(local.shape, F32),
            pltpu.SemaphoreType.DMA,
        ],
        compiler_params=params(32),
        name="attend",
    )(group, me, t_idx, noise_gen, noise_score, prev_latents, everyone, local)


def per_device(
    noise_gen,
    noise_score,
    prev_latents,
    t_idx,
    w_in,
    w_qkv,
    w_out,
    w_final,
    mod_scale,
    mod_shift,
    saved_features,
):
    groups = lax.axis_size("group")
    heads = lax.axis_size("seq")
    copies = lax.axis_size("dp")
    group = lax.axis_index("group").astype(jnp.int32).reshape(1)
    width = w_in.shape[2]

    operands = (
        prev_latents, noise_gen, noise_score, w_in, mod_scale, mod_shift,
        w_out[0].T, w_final[0].T, w_qkv[0].transpose(1, 0, 2),
    )
    sent, local = fold(group, t_idx, *operands)
    everyone = lax.all_gather(sent, "seq", axis=0, tiled=True).reshape(heads, ROWS, 128)

    me = lax.axis_index("seq").astype(jnp.int32).reshape(1)
    moved, prediction = attend(
        groups, group, me, t_idx, noise_gen, noise_score, prev_latents, everyone, local
    )
    moved = lax.all_to_all(moved, "group", 0, 0, tiled=True)

    quarter = width // groups
    whole = lambda *dims: pl.BlockSpec(dims, lambda n, g, t: (0,) * len(dims))
    parts = pl.pallas_call(
        partial_kernel,
        out_shape=shape_of((heads, 16, 512), BF16),
        grid_spec=pltpu.PrefetchScalarGridSpec(
            num_scalar_prefetch=2,
            grid=(1,),
            in_specs=[
                whole(groups, 64, 128),
                whole(2, 64, 64),
                whole(2, 64, 64),
                pl.BlockSpec((2, 64, quarter), lambda n, g, t: (0, 0, g[0])),
            ],
            out_specs=whole(heads, 16, 512),
        ),
        compiler_params=params(16),
        name="partial",
    )(group, t_idx, moved, noise_score, prev_latents, saved_features)
    parts = lax.all_to_all(parts, "seq", 0, 0, tiled=True)

    factor = 1.0 / math.sqrt(2 * copies * NTOK)
    summed, dmd_grad = pl.pallas_call(
        lambda *refs: scale_kernel(factor, *refs),
        out_shape=(shape_of((copies * 8, 384), BF16), shape_of((2, 64, 64), F32)),
        in_specs=[VECTOR] * 2,
        out_specs=(VECTOR, VECTOR),
        compiler_params=params(16),
        name="scale",
    )(parts, moved)
    summed = lax.all_to_all(summed, "dp", 0, 0, tiled=True)

    chips = heads // 2
    rows = pl.pallas_call(
        sum_kernel,
        out_shape=shape_of((groups * chips * 8, 384), BF16),
        in_specs=[VECTOR],
        out_specs=VECTOR,
        compiler_params=params(16),
        name="sum",
    )(summed)
    same_core = [
        [g * heads + 2 * y + core for g in range(groups) for y in range(chips)] for core in range(2)
    ]
    rows = lax.all_to_all(
        rows, ("group", "seq"), 0, 0, tiled=True, axis_index_groups=same_core
    )
    one_chip = [[2 * y, 2 * y + 1] for y in range(chips)]
    rows = lax.all_gather(rows, "seq", axis=0, tiled=True, axis_index_groups=one_chip)

    total = pl.pallas_call(
        place_kernel,
        out_shape=shape_of((64, width), F32),
        in_specs=[VECTOR],
        out_specs=VECTOR,
        compiler_params=params(16),
        name="place",
    )(rows)
    return prediction, dmd_grad, total.T


def solution(mesh):
    placed = (
        P("dp", "seq", None),
        P("dp", "seq", None),
        P("dp", "seq", None),
        P("dp"),
        P("group", None, None),
        P("group", None, None, "seq"),
        P("group", "seq", None),
        P("group", None, None),
        P("group", None),
        P("group", None),
        P("dp", "seq", None),
    )
    return jax.shard_map(
        per_device,
        mesh=mesh,
        in_specs=placed,
        out_specs=(P("group", "dp", "seq", None), P("dp", "seq", None), P()),
        check_vma=False,
    )
```

```python
import math

import jax
import jax.numpy as jnp
from jax import lax
from jax.experimental import pallas as pl
from jax.experimental.pallas import tpu as pltpu
from jax.sharding import PartitionSpec as P

NTOK = 1024
NOISE_LEVEL_COUNT = 1000
BF16 = jnp.bfloat16
F32 = jnp.float32
CHUNKS = 3
ROWS = 208


def dot(a, b, lhs=1, rhs=0):
    return lax.dot_general(a, b, (((lhs,), (rhs,)), ((), ())), preferred_element_type=F32)


def left_half(shape):
    return lax.broadcasted_iota(jnp.int32, shape, 1) < 64


def levels(t_ref):
    gen = jnp.where(lax.axis_index("group") == 0, 1.0, 0.0).astype(F32)
    level = [(t_ref[i].astype(F32) + 0.5) * (1.0 / NOISE_LEVEL_COUNT) for i in range(2)]
    return gen, level, [gen + (1.0 - gen) * value for value in level]


def level_rows(local_ref, lanes):
    rows = [local_ref[k : k + 1, 0:lanes] for k in range(136, 141)]
    return rows[0], rows[1:3], rows[3:5]


def noisy_latent(level, prev, noise):
    return (1.0 - level) * prev + level * noise.astype(F32)


def fold_kernel(*refs):
    sources, (sent_ref, own_ref, local_ref), held = refs[:10], refs[10:13], refs[13:23]
    left_ref, arrived = refs[23:]
    t_ref = held[9]
    width = sources[3].shape[2]
    step = width // CHUNKS
    pairs = [(sources[k], held[k]) for k in (9, 0, 1, 2, 4, 5, 6)]
    for at in range(0, width, step):
        part = pl.ds(at, step)
        pairs.append((sources[3].at[:, :, part], held[3].at[:, :, part]))
        pairs.append((sources[7].at[:, part], held[7].at[:, part]))
        pairs += [(sources[8].at[c, part], held[8].at[c, part]) for c in range(3)]
    loads = [pltpu.make_async_copy(*pair, arrived.at[k]) for k, pair in enumerate(pairs)]
    for load in loads:
        load.start()
    prev_ref, gen_ref, noise_ref, w_in_ref, scale_ref, shift_ref = held[:6]
    w_out_ref, w_final_ref, w_qkv_ref = held[6:9]
    for load in loads[:7]:
        load.wait()
    gen, level, used = levels(t_ref)
    latents = []
    for i in range(2):
        noisy = noisy_latent(level[i], prev_ref[i], noise_ref[i])
        latents.append(gen * gen_ref[i].astype(F32) + (1.0 - gen) * noisy)
    latent = jnp.concatenate(latents, axis=0).astype(BF16)
    squares = jnp.zeros((128, 128), F32)
    final = jnp.zeros((144, 64), F32)
    folded = [jnp.zeros((144, 128), F32) for _ in range(3)]
    row = lax.broadcasted_iota(jnp.int32, (16, step), 0)
    for n in range(CHUNKS):
        at = n * step
        for load in loads[7 + 5 * n : 12 + 5 * n]:
            load.wait()
        part = w_in_ref[0, :, at : at + step]
        projected = dot(latent, part)
        for lane in range(0, step, 128):
            piece = projected[:, lane : lane + 128]
            squares = squares + piece * piece
        shift = shift_ref[:, at : at + step]
        high = shift.astype(BF16).astype(F32)
        shifts = jnp.where(row == 0, high, jnp.where(row == 1, shift - high, 0.0))
        scaled = part.astype(F32) * scale_ref[:, at : at + step]
        left_ref[0:64, :] = part
        left_ref[64:128, :] = scaled.astype(BF16)
        left_ref[128:144, :] = shifts.astype(BF16)
        final = final + dot(left_ref[...], w_final_ref[:, at : at + step], 1, 1)
        for c in range(3):
            folded[c] = folded[c] + dot(left_ref[...], w_qkv_ref[c, at : at + step, :])
    mean = jnp.sum(squares, axis=1, keepdims=True) * (1.0 / width)
    scaled = (latent.astype(F32) * lax.rsqrt(mean + 1e-06)).astype(BF16)
    own = jnp.concatenate([scaled[0:64], scaled[64:128]], axis=1)
    sent_ref[144:208, :] = own
    own_ref[...] = own
    const = [part[128:129] + part[129:130] for part in folded]
    final_const = final[128:129] + final[129:130]
    factor = math.log2(math.e) / math.sqrt(128.0)
    w_out = w_out_ref[...]
    blocks, consts, locals_ = [], [], []
    value_const = dot(jnp.broadcast_to(const[2], (16, 128)).astype(BF16), w_out, 1, 1)
    for i in range(2):
        q, k, v = [(part[0:64] + used[i] * part[64:128]) for part in folded]
        kb = k.astype(BF16)
        scores = dot(q.astype(BF16), kb, 1, 1) * factor
        out = dot(v.astype(BF16), w_out, 1, 1)
        key_const = dot(jnp.broadcast_to(const[0], (16, 128)).astype(BF16), kb, 1, 1) * factor
        local = final[0:64] + used[i] * final[64:128]
        zero = jnp.zeros_like(local)
        if i == 0:
            blocks.append(jnp.concatenate([scores, out], axis=1))
            consts.append(jnp.concatenate([key_const, value_const], axis=1))
            locals_.append(jnp.concatenate([zero, local], axis=1))
        else:
            blocks.append(jnp.concatenate([out, scores], axis=1))
            consts.append(jnp.concatenate([value_const, key_const], axis=1))
            locals_.append(jnp.concatenate([local, zero], axis=1))
    sent_ref[0:64, :] = blocks[0].astype(BF16)
    sent_ref[64:128, :] = blocks[1].astype(BF16)
    row = lax.broadcasted_iota(jnp.int32, (16, 128), 0)
    sent_ref[128:144, :] = jnp.where(row == 0, consts[0], consts[1]).astype(BF16)
    local_ref[0:64, :] = locals_[0]
    local_ref[64:128, :] = locals_[1]
    both = jnp.concatenate([final_const, final_const], axis=1)
    local_ref[128:136, :] = jnp.broadcast_to(both, (8, 128))
    for k, value in enumerate([gen, *level, *used]):
        local_ref[136 + k : 137 + k, :] = jnp.full((1, 128), value, F32)


def attend_kernel(
    gen_ref, noise_ref, prev_ref, all_ref, own_ref, local_ref,
    moved_ref, prediction_ref, keys_ref, query_ref, mixed_ref,
):
    heads = all_ref.shape[0]
    gen, level, used = level_rows(local_ref, 64)
    for s in range(heads):
        keys_ref[64 * s : 64 * s + 64, 0:128] = all_ref[s, 144:208, :]
    keys_ref[:, 128:256] = jnp.ones((64 * heads, 128), BF16)
    left = left_half((64, 128))
    own = own_ref[...].astype(F32)
    stacked = jnp.concatenate([jnp.where(left, own, 0.0), jnp.where(left, 0.0, own)], axis=0)
    stacked = stacked.astype(BF16)
    const_sum = jnp.zeros((16, 128), F32)
    for h in range(heads):
        block = all_ref[h, 0:128, :]
        const = all_ref[h, 128:144, :].astype(F32)
        const_sum = const_sum + const
        query = dot(stacked, block)
        rows = slice(64 * h, 64 * h + 64)
        query_ref[0, rows, :] = jnp.where(left, query[0:64] + const[0:1], 0.0).astype(BF16)
        query_ref[1, rows, :] = jnp.where(left, 0.0, query[64:128] + const[1:2]).astype(BF16)
    step = 256
    wide_left = left_half((step, 128))
    for i in range(2):
        for at in range(0, 64 * heads, step):
            rows = slice(at, at + step)
            scores = dot(query_ref[i, rows, :], keys_ref[:, 0:128], 1, 1)
            top = jnp.max(scores, axis=1, keepdims=True)
            weights = jnp.exp2(scores - top).astype(BF16)
            mixed = dot(weights, keys_ref[...])
            mixed = mixed[:, 0:128] / mixed[:, 128:256]
            keep = wide_left if i == 0 else jnp.logical_not(wide_left)
            mixed_ref[i, rows, :] = jnp.where(keep, mixed, 0.0).astype(BF16)
    total = dot(stacked, local_ref[0:128, :].astype(BF16))
    for h in range(heads):
        rows = slice(64 * h, 64 * h + 64)
        pair = jnp.concatenate([mixed_ref[0, rows, :], mixed_ref[1, rows, :]], axis=0)
        total = total + dot(pair, all_ref[h, 0:128, :])
    wide = level_rows(local_ref, 128)[2]
    first = wide[0] * (total[0:64] + const_sum[0:1] + local_ref[128:129, :])
    second = wide[1] * (total[64:128] + const_sum[1:2] + local_ref[128:129, :])
    moved = jnp.where(left, second, first)
    for g in range(moved_ref.shape[0]):
        moved_ref[g] = moved.astype(BF16)
    for i, part in ((0, moved[:, 64:128]), (1, moved[:, 0:64])):
        noisy = noisy_latent(level[i], prev_ref[i], noise_ref[i])
        prediction_ref[0, i] = gen * gen_ref[i].astype(F32) + (1.0 - gen) * noisy - part


def guidance(moved_ref):
    return 2.5 * moved_ref[1].astype(F32) - 1.5 * moved_ref[2].astype(F32)


def partial_kernel(moved_ref, noise_ref, prev_ref, local_ref, saved_ref, out_ref):
    level = level_rows(local_ref, 64)[1]
    guided = guidance(moved_ref)
    down = moved_ref[3].astype(F32) - guided
    halves = (slice(64, 128), slice(0, 64))
    row = lax.broadcasted_iota(jnp.int32, (16, 128), 0)
    sums = []
    for i in range(2):
        real = noisy_latent(level[i], prev_ref[i], noise_ref[i]) - guided[:, halves[i]]
        gap = jnp.abs(prev_ref[i] - real)
        sums.append(jnp.sum(jnp.sum(gap, axis=0, keepdims=True), axis=1, keepdims=True))
    sums = jnp.where(row < 8, sums[0], sums[1])
    high = sums.astype(BF16).astype(F32)
    sums = jnp.where(left_half((16, 128)), high, sums - high).astype(BF16)
    tokens = jnp.concatenate([down[:, halves[0]], down[:, halves[1]]], axis=0).astype(BF16)
    out_row = lax.broadcasted_iota(jnp.int32, (128, 64), 0)
    channel = lax.broadcasted_iota(jnp.int32, (128, 64), 1)
    pick = jnp.where((out_row // 16) * 8 + out_row % 8 == channel, 1.0, 0.0).astype(BF16)
    spread_out = dot(pick, tokens, 1, 1)
    image = (lax.broadcasted_iota(jnp.int32, (128, 128), 0) % 16) // 8
    owner = lax.broadcasted_iota(jnp.int32, (128, 128), 1) // 64
    spread_out = jnp.where(image == owner, spread_out, 0.0).astype(BF16)
    lanes = pl.ds(pl.multiple_of(lax.axis_index("group") * 768, 128), 768)
    saved = jnp.concatenate([saved_ref[0, :, lanes], saved_ref[1, :, lanes]], axis=0)
    grad = dot(spread_out, saved).astype(BF16)
    for a in range(8):
        for b in range(2):
            out_ref[2 * a + b, :, 0:384] = grad[16 * a : 16 * a + 16, 384 * b : 384 * b + 384]
            out_ref[2 * a + b, :, 384:512] = sums


def scale_kernel(factor, part_ref, moved_ref, out_ref, grad_ref):
    total = part_ref[0].astype(F32)
    for s in range(1, part_ref.shape[0]):
        total = total + part_ref[s].astype(F32)
    spread = (total[:, 384:385] + total[:, 448:449]) * (1.0 / (NTOK * 64)) + 1e-05
    grad = total[:, 0:384] * (factor / spread)
    grad = grad[0:8] + grad[8:16]
    pair = jnp.concatenate([grad, grad], axis=0).astype(BF16)
    for at in range(0, out_ref.shape[0], 16):
        out_ref[at : at + 16, :] = pair
    gap = guidance(moved_ref) - moved_ref[3].astype(F32)
    grad_ref[0] = gap[:, 64:128] / spread[0:1]
    grad_ref[1] = gap[:, 0:64] / spread[8:9]


def sum_kernel(part_ref, out_ref):
    total = part_ref[0:16, :].astype(F32)
    for at in range(16, part_ref.shape[0], 16):
        total = total + part_ref[at : at + 16, :].astype(F32)
    total = total[0:8] + total[8:16]
    pair = jnp.concatenate([total, total], axis=0).astype(BF16)
    for at in range(0, out_ref.shape[0], 16):
        out_ref[at : at + 16, :] = pair


def place_kernel(part_ref, out_ref):
    at = 0
    for core in range(2):
        for g in range(4):
            lanes = slice(768 * g + 384 * core, 768 * g + 384 * core + 384)
            for row in range(0, 64, 16):
                out_ref[row : row + 16, lanes] = part_ref[at : at + 16, :].astype(F32)
                at += 16


VECTOR = pl.BlockSpec(memory_space=pltpu.VMEM)


def params(mib):
    return pltpu.CompilerParams(vmem_limit_bytes=mib << 20)


def shape_of(shape, dtype):
    return jax.ShapeDtypeStruct(shape, dtype)


def fold(*operands):
    width = operands[3].shape[2]
    return pl.pallas_call(
        fold_kernel,
        out_shape=(
            shape_of((ROWS, 128), BF16), pltpu.VMEM((64, 128), BF16), pltpu.VMEM((144, 128), F32)
        ),
        in_specs=[pl.BlockSpec(memory_space=pl.ANY)] * len(operands),
        out_specs=(VECTOR, VECTOR, VECTOR),
        scratch_shapes=[pltpu.VMEM(x.shape, x.dtype) for x in operands[:9]]
        + [
            pltpu.SMEM(operands[9].shape, jnp.int32),
            pltpu.VMEM((144, width // CHUNKS), BF16),
            pltpu.SemaphoreType.DMA((7 + 5 * CHUNKS,)),
        ],
        compiler_params=params(58),
        name="fold",
    )(*operands)


def attend(groups, *operands):
    heads = operands[3].shape[0]
    return pl.pallas_call(
        attend_kernel,
        out_shape=(shape_of((groups, 64, 128), BF16), shape_of((1, 2, 64, 64), F32)),
        in_specs=[VECTOR] * 6,
        out_specs=(VECTOR, VECTOR),
        scratch_shapes=[
            pltpu.VMEM((64 * heads, 256), BF16),
            pltpu.VMEM((2, 64 * heads, 128), BF16),
            pltpu.VMEM((2, 64 * heads, 128), BF16),
        ],
        compiler_params=params(32),
        name="attend",
    )(*operands)


def per_device(
    noise_gen,
    noise_score,
    prev_latents,
    t_idx,
    w_in,
    w_qkv,
    w_out,
    w_final,
    mod_scale,
    mod_shift,
    saved_features,
):
    groups = lax.axis_size("group")
    heads = lax.axis_size("seq")
    copies = lax.axis_size("dp")
    width = w_in.shape[2]

    sent, own, local = fold(
        prev_latents, noise_gen, noise_score, w_in, mod_scale, mod_shift,
        w_out[0].T, w_final[0].T, w_qkv[0].transpose(1, 0, 2), t_idx,
    )
    everyone = lax.all_gather(sent, "seq", axis=0, tiled=True).reshape(heads, ROWS, 128)

    moved, prediction = attend(
        groups, noise_gen, noise_score, prev_latents, everyone, own, local
    )
    moved = lax.all_to_all(moved, "group", 0, 0, tiled=True)

    parts = pl.pallas_call(
        partial_kernel,
        out_shape=shape_of((heads, 16, 512), BF16),
        in_specs=[VECTOR] * 5,
        out_specs=VECTOR,
        compiler_params=params(16),
        name="partial",
    )(moved, noise_score, prev_latents, local, saved_features)
    parts = lax.all_to_all(parts, "seq", 0, 0, tiled=True)

    factor = 1.0 / math.sqrt(2 * copies * NTOK)
    summed, dmd_grad = pl.pallas_call(
        lambda *refs: scale_kernel(factor, *refs),
        out_shape=(shape_of((copies * 8, 384), BF16), shape_of((2, 64, 64), F32)),
        in_specs=[VECTOR] * 2,
        out_specs=(VECTOR, VECTOR),
        compiler_params=params(16),
        name="scale",
    )(parts, moved)
    summed = lax.all_to_all(summed, "dp", 0, 0, tiled=True)

    chips = heads // 2
    rows = pl.pallas_call(
        sum_kernel,
        out_shape=shape_of((groups * chips * 8, 384), BF16),
        in_specs=[VECTOR],
        out_specs=VECTOR,
        compiler_params=params(16),
        name="sum",
    )(summed)
    same_core = [
        [g * heads + 2 * y + core for g in range(groups) for y in range(chips)] for core in range(2)
    ]
    rows = lax.all_to_all(
        rows, ("group", "seq"), 0, 0, tiled=True, axis_index_groups=same_core
    )
    one_chip = [[2 * y, 2 * y + 1] for y in range(chips)]
    rows = lax.all_gather(rows, "seq", axis=0, tiled=True, axis_index_groups=one_chip)

    total = pl.pallas_call(
        place_kernel,
        out_shape=shape_of((64, width), F32),
        in_specs=[VECTOR],
        out_specs=VECTOR,
        compiler_params=params(16),
        name="place",
    )(rows)
    return prediction, dmd_grad, total.T


def solution(mesh):
    placed = (
        P("dp", "seq", None),
        P("dp", "seq", None),
        P("dp", "seq", None),
        P("dp"),
        P("group", None, None),
        P("group", None, None, "seq"),
        P("group", "seq", None),
        P("group", None, None),
        P("group", None),
        P("group", None),
        P("dp", "seq", None),
    )
    return jax.shard_map(
        per_device,
        mesh=mesh,
        in_specs=placed,
        out_specs=(P("group", "dp", "seq", None), P("dp", "seq", None), P()),
        check_vma=False,
    )
```

```python
import math

import jax
import jax.numpy as jnp
from jax import lax
from jax.experimental import pallas as pl
from jax.experimental.pallas import tpu as pltpu
from jax.sharding import PartitionSpec as P

NTOK = 1024
NOISE_LEVEL_COUNT = 1000
BF16 = jnp.bfloat16
F32 = jnp.float32
CHUNKS = 3
ROWS = 208


def dot(a, b, lhs=1, rhs=0):
    return lax.dot_general(a, b, (((lhs,), (rhs,)), ((), ())), preferred_element_type=F32)


def left_half(shape):
    return lax.broadcasted_iota(jnp.int32, shape, 1) < 64


def levels(t_ref):
    gen = jnp.where(lax.axis_index("group") == 0, 1.0, 0.0).astype(F32)
    level = [(t_ref[i].astype(F32) + 0.5) * (1.0 / NOISE_LEVEL_COUNT) for i in range(2)]
    return gen, level, [gen + (1.0 - gen) * value for value in level]


def level_rows(local_ref, lanes):
    rows = [local_ref[k : k + 1, 0:lanes] for k in range(136, 141)]
    return rows[0], rows[1:3], rows[3:5]


def noisy_latent(level, prev, noise):
    return (1.0 - level) * prev + level * noise.astype(F32)


def fold_kernel(*refs):
    sources, (sent_ref, own_ref, local_ref), held = refs[:10], refs[10:13], refs[13:23]
    left_ref, arrived = refs[23:]
    t_ref = held[9]
    width = sources[3].shape[2]
    step = width // CHUNKS
    pairs = [(sources[k], held[k]) for k in (9, 0, 1, 2, 4, 5, 6)]
    for at in range(0, width, step):
        part = pl.ds(at, step)
        pairs.append((sources[3].at[:, :, part], held[3].at[:, :, part]))
        pairs.append((sources[7].at[:, part], held[7].at[:, part]))
        pairs += [(sources[8].at[c, part], held[8].at[c, part]) for c in range(3)]
    loads = [pltpu.make_async_copy(*pair, arrived.at[k]) for k, pair in enumerate(pairs)]
    for load in loads:
        load.start()
    prev_ref, gen_ref, noise_ref, w_in_ref, scale_ref, shift_ref = held[:6]
    w_out_ref, w_final_ref, w_qkv_ref = held[6:9]
    for load in loads[:7]:
        load.wait()
    gen, level, used = levels(t_ref)
    latents = []
    for i in range(2):
        noisy = noisy_latent(level[i], prev_ref[i], noise_ref[i])
        latents.append(gen * gen_ref[i].astype(F32) + (1.0 - gen) * noisy)
    latent = jnp.concatenate(latents, axis=0).astype(BF16)
    squares = jnp.zeros((128, 128), F32)
    final = jnp.zeros((144, 64), F32)
    folded = [jnp.zeros((144, 128), F32) for _ in range(3)]
    row = lax.broadcasted_iota(jnp.int32, (16, step), 0)
    for n in range(CHUNKS):
        at = n * step
        for load in loads[7 + 5 * n : 12 + 5 * n]:
            load.wait()
        part = w_in_ref[0, :, at : at + step]
        projected = dot(latent, part)
        for lane in range(0, step, 128):
            piece = projected[:, lane : lane + 128]
            squares = squares + piece * piece
        shift = shift_ref[:, at : at + step]
        high = shift.astype(BF16).astype(F32)
        shifts = jnp.where(row == 0, high, jnp.where(row == 1, shift - high, 0.0))
        scaled = part.astype(F32) * scale_ref[:, at : at + step]
        left_ref[0:64, :] = part
        left_ref[64:128, :] = scaled.astype(BF16)
        left_ref[128:144, :] = shifts.astype(BF16)
        final = final + dot(left_ref[...], w_final_ref[:, at : at + step], 1, 1)
        for c in range(3):
            folded[c] = folded[c] + dot(left_ref[...], w_qkv_ref[c, at : at + step, :])
    mean = jnp.sum(squares, axis=1, keepdims=True) * (1.0 / width)
    scaled = (latent.astype(F32) * lax.rsqrt(mean + 1e-06)).astype(BF16)
    own = jnp.concatenate([scaled[0:64], scaled[64:128]], axis=1)
    sent_ref[144:208, :] = own
    own_ref[...] = own
    const = [part[128:129] + part[129:130] for part in folded]
    final_const = final[128:129] + final[129:130]
    factor = math.log2(math.e) / math.sqrt(128.0)
    w_out = w_out_ref[...]
    blocks, consts, locals_ = [], [], []
    value_const = dot(jnp.broadcast_to(const[2], (16, 128)).astype(BF16), w_out, 1, 1)
    for i in range(2):
        q, k, v = [(part[0:64] + used[i] * part[64:128]) for part in folded]
        kb = k.astype(BF16)
        scores = dot(q.astype(BF16), kb, 1, 1) * factor
        out = dot(v.astype(BF16), w_out, 1, 1)
        key_const = dot(jnp.broadcast_to(const[0], (16, 128)).astype(BF16), kb, 1, 1) * factor
        local = final[0:64] + used[i] * final[64:128]
        zero = jnp.zeros_like(local)
        if i == 0:
            blocks.append(jnp.concatenate([scores, out], axis=1))
            consts.append(jnp.concatenate([key_const, value_const], axis=1))
            locals_.append(jnp.concatenate([zero, local], axis=1))
        else:
            blocks.append(jnp.concatenate([out, scores], axis=1))
            consts.append(jnp.concatenate([value_const, key_const], axis=1))
            locals_.append(jnp.concatenate([local, zero], axis=1))
    sent_ref[0:64, :] = blocks[0].astype(BF16)
    sent_ref[64:128, :] = blocks[1].astype(BF16)
    row = lax.broadcasted_iota(jnp.int32, (16, 128), 0)
    sent_ref[128:144, :] = jnp.where(row == 0, consts[0], consts[1]).astype(BF16)
    local_ref[0:64, :] = locals_[0]
    local_ref[64:128, :] = locals_[1]
    both = jnp.concatenate([final_const, final_const], axis=1)
    local_ref[128:136, :] = jnp.broadcast_to(both, (8, 128))
    for k, value in enumerate([gen, *level, *used]):
        local_ref[136 + k : 137 + k, :] = jnp.full((1, 128), value, F32)


def attend_kernel(
    gen_ref, noise_ref, prev_ref, all_ref, own_ref, local_ref,
    moved_ref, prediction_ref, keys_ref, query_ref, mixed_ref,
):
    heads = all_ref.shape[0]
    gen, level, used = level_rows(local_ref, 64)
    for s in range(heads):
        keys_ref[64 * s : 64 * s + 64, 0:128] = all_ref[s, 144:208, :]
    keys_ref[:, 128:256] = jnp.ones((64 * heads, 128), BF16)
    left = left_half((64, 128))
    own = own_ref[...].astype(F32)
    stacked = jnp.concatenate([jnp.where(left, own, 0.0), jnp.where(left, 0.0, own)], axis=0)
    stacked = stacked.astype(BF16)
    const_sum = jnp.zeros((16, 128), F32)
    for h in range(heads):
        block = all_ref[h, 0:128, :]
        const = all_ref[h, 128:144, :].astype(F32)
        const_sum = const_sum + const
        query = dot(stacked, block)
        rows = slice(64 * h, 64 * h + 64)
        query_ref[0, rows, :] = jnp.where(left, query[0:64] + const[0:1], 0.0).astype(BF16)
        query_ref[1, rows, :] = jnp.where(left, 0.0, query[64:128] + const[1:2]).astype(BF16)
    step = 256
    wide_left = left_half((step, 128))
    for i in range(2):
        for at in range(0, 64 * heads, step):
            rows = slice(at, at + step)
            scores = dot(query_ref[i, rows, :], keys_ref[:, 0:128], 1, 1)
            top = jnp.max(scores, axis=1, keepdims=True)
            weights = jnp.exp2(scores - top).astype(BF16)
            mixed = dot(weights, keys_ref[...])
            mixed = mixed[:, 0:128] / mixed[:, 128:256]
            keep = wide_left if i == 0 else jnp.logical_not(wide_left)
            mixed_ref[i, rows, :] = jnp.where(keep, mixed, 0.0).astype(BF16)
    total = dot(stacked, local_ref[0:128, :].astype(BF16))
    for h in range(heads):
        rows = slice(64 * h, 64 * h + 64)
        pair = jnp.concatenate([mixed_ref[0, rows, :], mixed_ref[1, rows, :]], axis=0)
        total = total + dot(pair, all_ref[h, 0:128, :])
    wide = level_rows(local_ref, 128)[2]
    first = wide[0] * (total[0:64] + const_sum[0:1] + local_ref[128:129, :])
    second = wide[1] * (total[64:128] + const_sum[1:2] + local_ref[128:129, :])
    moved = jnp.where(left, second, first)
    for g in range(moved_ref.shape[0]):
        moved_ref[g] = moved.astype(BF16)
    for i, part in ((0, moved[:, 64:128]), (1, moved[:, 0:64])):
        noisy = noisy_latent(level[i], prev_ref[i], noise_ref[i])
        prediction_ref[0, i] = gen * gen_ref[i].astype(F32) + (1.0 - gen) * noisy - part


def guidance(moved_ref):
    return 2.5 * moved_ref[1].astype(F32) - 1.5 * moved_ref[2].astype(F32)


def partial_kernel(moved_ref, noise_ref, prev_ref, local_ref, saved_ref, out_ref):
    level = level_rows(local_ref, 64)[1]
    guided = guidance(moved_ref)
    down = moved_ref[3].astype(F32) - guided
    halves = (slice(64, 128), slice(0, 64))
    row = lax.broadcasted_iota(jnp.int32, (16, 128), 0)
    sums = []
    for i in range(2):
        real = noisy_latent(level[i], prev_ref[i], noise_ref[i]) - guided[:, halves[i]]
        gap = jnp.abs(prev_ref[i] - real)
        sums.append(jnp.sum(jnp.sum(gap, axis=0, keepdims=True), axis=1, keepdims=True))
    sums = jnp.where(row < 8, sums[0], sums[1])
    high = sums.astype(BF16).astype(F32)
    sums = jnp.where(left_half((16, 128)), high, sums - high).astype(BF16)
    tokens = jnp.concatenate([down[:, halves[0]], down[:, halves[1]]], axis=0).astype(BF16)
    out_row = lax.broadcasted_iota(jnp.int32, (128, 64), 0)
    channel = lax.broadcasted_iota(jnp.int32, (128, 64), 1)
    pick = jnp.where((out_row // 16) * 8 + out_row % 8 == channel, 1.0, 0.0).astype(BF16)
    spread_out = dot(pick, tokens, 1, 1)
    image = (lax.broadcasted_iota(jnp.int32, (128, 128), 0) % 16) // 8
    owner = lax.broadcasted_iota(jnp.int32, (128, 128), 1) // 64
    spread_out = jnp.where(image == owner, spread_out, 0.0).astype(BF16)
    lanes = pl.ds(pl.multiple_of(lax.axis_index("group") * 768, 128), 768)
    saved = jnp.concatenate([saved_ref[0, :, lanes], saved_ref[1, :, lanes]], axis=0)
    grad = dot(spread_out, saved).astype(BF16)
    for a in range(8):
        for b in range(2):
            out_ref[2 * a + b, :, 0:384] = grad[16 * a : 16 * a + 16, 384 * b : 384 * b + 384]
            out_ref[2 * a + b, :, 384:512] = sums


def scale_kernel(factor, part_ref, moved_ref, out_ref, grad_ref):
    total = part_ref[0].astype(F32)
    for s in range(1, part_ref.shape[0]):
        total = total + part_ref[s].astype(F32)
    spread = (total[:, 384:385] + total[:, 448:449]) * (1.0 / (NTOK * 64)) + 1e-05
    grad = total[:, 0:384] * (factor / spread)
    grad = grad[0:8] + grad[8:16]
    pair = jnp.concatenate([grad, grad], axis=0).astype(BF16)
    for at in range(0, out_ref.shape[0], 16):
        out_ref[at : at + 16, :] = pair
    gap = guidance(moved_ref) - moved_ref[3].astype(F32)
    grad_ref[0] = gap[:, 64:128] / spread[0:1]
    grad_ref[1] = gap[:, 0:64] / spread[8:9]


def sum_kernel(part_ref, out_ref):
    total = part_ref[0:16, :].astype(F32)
    for at in range(16, part_ref.shape[0], 16):
        total = total + part_ref[at : at + 16, :].astype(F32)
    total = total[0:8] + total[8:16]
    pair = jnp.concatenate([total, total], axis=0).astype(BF16)
    for at in range(0, out_ref.shape[0], 16):
        out_ref[at : at + 16, :] = pair


def place_kernel(
    part_ref, prediction_ref, grad_ref, out_ref, prediction_out, grad_out, wide_ref, done
):
    stores = [
        pltpu.make_async_copy(prediction_ref, prediction_out, done.at[8]),
        pltpu.make_async_copy(grad_ref, grad_out, done.at[9]),
    ]
    for store in stores:
        store.start()
    at = 0
    for core in range(2):
        for g in range(4):
            lanes = pl.ds(768 * g + 384 * core, 384)
            for row in range(0, 64, 16):
                wide_ref[row : row + 16, lanes] = part_ref[at : at + 16, :].astype(F32)
                at += 16
            source, target = wide_ref.at[:, lanes], out_ref.at[:, lanes]
            stores.append(pltpu.make_async_copy(source, target, done.at[4 * core + g]))
            stores[-1].start()
    for store in stores:
        store.wait()


VECTOR = pl.BlockSpec(memory_space=pltpu.VMEM)


def params(mib):
    return pltpu.CompilerParams(vmem_limit_bytes=mib << 20)


def shape_of(shape, dtype):
    return jax.ShapeDtypeStruct(shape, dtype)


def fold(*operands):
    width = operands[3].shape[2]
    return pl.pallas_call(
        fold_kernel,
        out_shape=(
            pltpu.VMEM((ROWS, 128), BF16), pltpu.VMEM((64, 128), BF16), pltpu.VMEM((144, 128), F32)
        ),
        in_specs=[pl.BlockSpec(memory_space=pl.ANY)] * len(operands),
        out_specs=(VECTOR, VECTOR, VECTOR),
        scratch_shapes=[pltpu.VMEM(x.shape, x.dtype) for x in operands[:9]]
        + [
            pltpu.SMEM(operands[9].shape, jnp.int32),
            pltpu.VMEM((144, width // CHUNKS), BF16),
            pltpu.SemaphoreType.DMA((7 + 5 * CHUNKS,)),
        ],
        compiler_params=params(58),
        name="fold",
    )(*operands)


def attend(groups, *operands):
    heads = operands[3].shape[0]
    return pl.pallas_call(
        attend_kernel,
        out_shape=(shape_of((groups, 64, 128), BF16), pltpu.VMEM((1, 2, 64, 64), F32)),
        in_specs=[VECTOR] * 6,
        out_specs=(VECTOR, VECTOR),
        scratch_shapes=[
            pltpu.VMEM((64 * heads, 256), BF16),
            pltpu.VMEM((2, 64 * heads, 128), BF16),
            pltpu.VMEM((2, 64 * heads, 128), BF16),
        ],
        compiler_params=params(32),
        name="attend",
    )(*operands)


def per_device(
    noise_gen,
    noise_score,
    prev_latents,
    t_idx,
    w_in,
    w_qkv,
    w_out,
    w_final,
    mod_scale,
    mod_shift,
    saved_features,
):
    groups = lax.axis_size("group")
    heads = lax.axis_size("seq")
    copies = lax.axis_size("dp")
    width = w_in.shape[2]

    sent, own, local = fold(
        prev_latents, noise_gen, noise_score, w_in, mod_scale, mod_shift,
        w_out[0].T, w_final[0].T, w_qkv[0].transpose(1, 0, 2), t_idx,
    )
    everyone = lax.all_gather(sent, "seq", axis=0, tiled=True).reshape(heads, ROWS, 128)

    moved, prediction = attend(
        groups, noise_gen, noise_score, prev_latents, everyone, own, local
    )
    moved = lax.all_to_all(moved, "group", 0, 0, tiled=True)

    parts = pl.pallas_call(
        partial_kernel,
        out_shape=shape_of((heads, 16, 512), BF16),
        in_specs=[VECTOR] * 5,
        out_specs=VECTOR,
        compiler_params=params(16),
        name="partial",
    )(moved, noise_score, prev_latents, local, saved_features)
    parts = lax.all_to_all(parts, "seq", 0, 0, tiled=True)

    factor = 1.0 / math.sqrt(2 * copies * NTOK)
    summed, dmd_grad = pl.pallas_call(
        lambda *refs: scale_kernel(factor, *refs),
        out_shape=(shape_of((copies * 8, 384), BF16), pltpu.VMEM((2, 64, 64), F32)),
        in_specs=[VECTOR] * 2,
        out_specs=(VECTOR, VECTOR),
        compiler_params=params(16),
        name="scale",
    )(parts, moved)
    summed = lax.all_to_all(summed, "dp", 0, 0, tiled=True)

    chips = heads // 2
    rows = pl.pallas_call(
        sum_kernel,
        out_shape=shape_of((groups * chips * 8, 384), BF16),
        in_specs=[VECTOR],
        out_specs=VECTOR,
        compiler_params=params(16),
        name="sum",
    )(summed)
    same_core = [
        [g * heads + 2 * y + core for g in range(groups) for y in range(chips)] for core in range(2)
    ]
    rows = lax.all_to_all(
        rows, ("group", "seq"), 0, 0, tiled=True, axis_index_groups=same_core
    )
    one_chip = [[2 * y, 2 * y + 1] for y in range(chips)]
    rows = lax.all_gather(rows, "seq", axis=0, tiled=True, axis_index_groups=one_chip)

    total, prediction, dmd_grad = pl.pallas_call(
        place_kernel,
        out_shape=(
            shape_of((64, width), F32), shape_of(prediction.shape, F32), shape_of(dmd_grad.shape, F32)
        ),
        in_specs=[VECTOR] * 3,
        out_specs=(pl.BlockSpec(memory_space=pl.ANY),) * 3,
        scratch_shapes=[pltpu.VMEM((64, width), F32), pltpu.SemaphoreType.DMA((10,))],
        compiler_params=params(16),
        name="place",
    )(rows, prediction, dmd_grad)
    return prediction, dmd_grad, total.T


def solution(mesh):
    placed = (
        P("dp", "seq", None),
        P("dp", "seq", None),
        P("dp", "seq", None),
        P("dp"),
        P("group", None, None),
        P("group", None, None, "seq"),
        P("group", "seq", None),
        P("group", None, None),
        P("group", None),
        P("group", None),
        P("dp", "seq", None),
    )
    return jax.shard_map(
        per_device,
        mesh=mesh,
        in_specs=placed,
        out_specs=(P("group", "dp", "seq", None), P("dp", "seq", None), P()),
        check_vma=False,
    )
```

```python
import math

import jax
import jax.numpy as jnp
from jax import lax
from jax.experimental import pallas as pl
from jax.experimental.pallas import tpu as pltpu
from jax.sharding import PartitionSpec as P

NTOK = 1024
NOISE_LEVEL_COUNT = 1000
BF16 = jnp.bfloat16
F32 = jnp.float32
CHUNKS = 3
ROWS = 208


def dot(a, b, lhs=1, rhs=0):
    return lax.dot_general(a, b, (((lhs,), (rhs,)), ((), ())), preferred_element_type=F32)


def left_half(shape):
    return lax.broadcasted_iota(jnp.int32, shape, 1) < 64


def levels(t_ref):
    gen = jnp.where(lax.axis_index("group") == 0, 1.0, 0.0).astype(F32)
    level = [(t_ref[i].astype(F32) + 0.5) * (1.0 / NOISE_LEVEL_COUNT) for i in range(2)]
    return gen, level, [gen + (1.0 - gen) * value for value in level]


def level_rows(local_ref, lanes):
    rows = [local_ref[k : k + 1, 0:lanes] for k in range(136, 141)]
    return rows[0], rows[1:3], rows[3:5]


def noisy_latent(level, prev, noise):
    return (1.0 - level) * prev + level * noise.astype(F32)


def fold_kernel(*refs):
    sources, (sent_ref, own_ref, local_ref), held = refs[:10], refs[10:13], refs[13:23]
    left_ref, arrived = refs[23:]
    t_ref = held[9]
    width = sources[3].shape[2]
    step = width // CHUNKS
    pairs = [(sources[k], held[k]) for k in (9, 0, 1, 2, 4, 5, 6)]
    for at in range(0, width, step):
        part = pl.ds(at, step)
        pairs.append((sources[3].at[:, :, part], held[3].at[:, :, part]))
        pairs.append((sources[7].at[:, part], held[7].at[:, part]))
        pairs += [(sources[8].at[c, part], held[8].at[c, part]) for c in range(3)]
    loads = [pltpu.make_async_copy(*pair, arrived.at[k]) for k, pair in enumerate(pairs)]
    for load in loads:
        load.start()
    prev_ref, gen_ref, noise_ref, w_in_ref, scale_ref, shift_ref = held[:6]
    w_out_ref, w_final_ref, w_qkv_ref = held[6:9]
    for load in loads[:7]:
        load.wait()
    gen, level, used = levels(t_ref)
    latents = []
    for i in range(2):
        noisy = noisy_latent(level[i], prev_ref[i], noise_ref[i])
        latents.append(gen * gen_ref[i].astype(F32) + (1.0 - gen) * noisy)
    latent = jnp.concatenate(latents, axis=0).astype(BF16)
    squares = jnp.zeros((128, 128), F32)
    final = jnp.zeros((144, 64), F32)
    folded = [jnp.zeros((144, 128), F32) for _ in range(3)]
    row = lax.broadcasted_iota(jnp.int32, (16, step), 0)
    for n in range(CHUNKS):
        at = n * step
        for load in loads[7 + 5 * n : 12 + 5 * n]:
            load.wait()
        part = w_in_ref[0, :, at : at + step]
        projected = dot(latent, part)
        for lane in range(0, step, 128):
            piece = projected[:, lane : lane + 128]
            squares = squares + piece * piece
        shift = shift_ref[:, at : at + step]
        high = shift.astype(BF16).astype(F32)
        shifts = jnp.where(row == 0, high, jnp.where(row == 1, shift - high, 0.0))
        scaled = part.astype(F32) * scale_ref[:, at : at + step]
        left_ref[0:64, :] = part
        left_ref[64:128, :] = scaled.astype(BF16)
        left_ref[128:144, :] = shifts.astype(BF16)
        final = final + dot(left_ref[...], w_final_ref[:, at : at + step], 1, 1)
        for c in range(3):
            folded[c] = folded[c] + dot(left_ref[...], w_qkv_ref[c, at : at + step, :])
    mean = jnp.sum(squares, axis=1, keepdims=True) * (1.0 / width)
    scaled = (latent.astype(F32) * lax.rsqrt(mean + 1e-06)).astype(BF16)
    own = jnp.concatenate([scaled[0:64], scaled[64:128]], axis=1)
    sent_ref[144:208, :] = own
    own_ref[...] = own
    const = [part[128:129] + part[129:130] for part in folded]
    final_const = final[128:129] + final[129:130]
    factor = math.log2(math.e) / math.sqrt(128.0)
    w_out = w_out_ref[...]
    blocks, consts, locals_ = [], [], []
    value_const = dot(jnp.broadcast_to(const[2], (16, 128)).astype(BF16), w_out, 1, 1)
    for i in range(2):
        q, k, v = [(part[0:64] + used[i] * part[64:128]) for part in folded]
        kb = k.astype(BF16)
        scores = dot(q.astype(BF16), kb, 1, 1) * factor
        out = dot(v.astype(BF16), w_out, 1, 1)
        key_const = dot(jnp.broadcast_to(const[0], (16, 128)).astype(BF16), kb, 1, 1) * factor
        local = final[0:64] + used[i] * final[64:128]
        zero = jnp.zeros_like(local)
        if i == 0:
            blocks.append(jnp.concatenate([scores, out], axis=1))
            consts.append(jnp.concatenate([key_const, value_const], axis=1))
            locals_.append(jnp.concatenate([zero, local], axis=1))
        else:
            blocks.append(jnp.concatenate([out, scores], axis=1))
            consts.append(jnp.concatenate([value_const, key_const], axis=1))
            locals_.append(jnp.concatenate([local, zero], axis=1))
    sent_ref[0:64, :] = blocks[0].astype(BF16)
    sent_ref[64:128, :] = blocks[1].astype(BF16)
    row = lax.broadcasted_iota(jnp.int32, (16, 128), 0)
    sent_ref[128:144, :] = jnp.where(row == 0, consts[0], consts[1]).astype(BF16)
    local_ref[0:64, :] = locals_[0]
    local_ref[64:128, :] = locals_[1]
    both = jnp.concatenate([final_const, final_const], axis=1)
    local_ref[128:136, :] = jnp.broadcast_to(both, (8, 128))
    for k, value in enumerate([gen, *level, *used]):
        local_ref[136 + k : 137 + k, :] = jnp.full((1, 128), value, F32)


def attend_kernel(
    gen_ref, noise_ref, prev_ref, all_ref, own_ref, local_ref,
    moved_ref, prediction_ref, keys_ref, query_ref, mixed_ref,
):
    heads = all_ref.shape[0]
    gen, level, used = level_rows(local_ref, 64)
    for s in range(heads):
        keys_ref[64 * s : 64 * s + 64, 0:128] = all_ref[s, 144:208, :]
    keys_ref[:, 128:256] = jnp.ones((64 * heads, 128), BF16)
    left = left_half((64, 128))
    own = own_ref[...].astype(F32)
    stacked = jnp.concatenate([jnp.where(left, own, 0.0), jnp.where(left, 0.0, own)], axis=0)
    stacked = stacked.astype(BF16)
    const_sum = jnp.zeros((16, 128), F32)
    for h in range(heads):
        block = all_ref[h, 0:128, :]
        const = all_ref[h, 128:144, :].astype(F32)
        const_sum = const_sum + const
        query = dot(stacked, block)
        rows = slice(64 * h, 64 * h + 64)
        query_ref[0, rows, :] = jnp.where(left, query[0:64] + const[0:1], 0.0).astype(BF16)
        query_ref[1, rows, :] = jnp.where(left, 0.0, query[64:128] + const[1:2]).astype(BF16)
    step = 256
    wide_left = left_half((step, 128))
    for i in range(2):
        for at in range(0, 64 * heads, step):
            rows = slice(at, at + step)
            scores = dot(query_ref[i, rows, :], keys_ref[:, 0:128], 1, 1)
            top = jnp.max(scores, axis=1, keepdims=True)
            weights = jnp.exp2(scores - top).astype(BF16)
            mixed = dot(weights, keys_ref[...])
            mixed = mixed[:, 0:128] / mixed[:, 128:256]
            keep = wide_left if i == 0 else jnp.logical_not(wide_left)
            mixed_ref[i, rows, :] = jnp.where(keep, mixed, 0.0).astype(BF16)
    total = dot(stacked, local_ref[0:128, :].astype(BF16))
    for h in range(heads):
        rows = slice(64 * h, 64 * h + 64)
        pair = jnp.concatenate([mixed_ref[0, rows, :], mixed_ref[1, rows, :]], axis=0)
        total = total + dot(pair, all_ref[h, 0:128, :])
    wide = level_rows(local_ref, 128)[2]
    first = wide[0] * (total[0:64] + const_sum[0:1] + local_ref[128:129, :])
    second = wide[1] * (total[64:128] + const_sum[1:2] + local_ref[128:129, :])
    moved = jnp.where(left, second, first)
    for g in range(moved_ref.shape[0]):
        moved_ref[g] = moved.astype(BF16)
    for i, part in ((0, moved[:, 64:128]), (1, moved[:, 0:64])):
        noisy = noisy_latent(level[i], prev_ref[i], noise_ref[i])
        prediction_ref[0, i] = gen * gen_ref[i].astype(F32) + (1.0 - gen) * noisy - part


def guidance(moved_ref):
    return 2.5 * moved_ref[1].astype(F32) - 1.5 * moved_ref[2].astype(F32)


def partial_kernel(moved_ref, noise_ref, prev_ref, local_ref, saved_ref, keep_ref, give_ref):
    level = level_rows(local_ref, 64)[1]
    guided = guidance(moved_ref)
    down = moved_ref[3].astype(F32) - guided
    halves = (slice(64, 128), slice(0, 64))
    row = lax.broadcasted_iota(jnp.int32, (16, 128), 0)
    sums = []
    for i in range(2):
        real = noisy_latent(level[i], prev_ref[i], noise_ref[i]) - guided[:, halves[i]]
        gap = jnp.abs(prev_ref[i] - real)
        sums.append(jnp.sum(jnp.sum(gap, axis=0, keepdims=True), axis=1, keepdims=True))
    sums = jnp.where(row < 8, sums[0], sums[1])
    tokens = jnp.concatenate([down[:, halves[0]], down[:, halves[1]]], axis=0).astype(BF16)
    out_row = lax.broadcasted_iota(jnp.int32, (128, 64), 0)
    channel = lax.broadcasted_iota(jnp.int32, (128, 64), 1)
    pick = jnp.where((out_row // 16) * 8 + out_row % 8 == channel, 1.0, 0.0).astype(BF16)
    spread_out = dot(pick, tokens, 1, 1)
    image = (lax.broadcasted_iota(jnp.int32, (128, 128), 0) % 16) // 8
    owner = lax.broadcasted_iota(jnp.int32, (128, 128), 1) // 64
    spread_out = jnp.where(image == owner, spread_out, 0.0).astype(BF16)
    core = lax.rem(lax.axis_index("seq"), 2)
    for half, ref in ((1 - core, give_ref), (core, keep_ref)):
        first = lax.axis_index("group") * 768 + half * 384
        lanes = pl.ds(pl.multiple_of(first, 128), 384)
        saved = jnp.concatenate([saved_ref[0, :, lanes], saved_ref[1, :, lanes]], axis=0)
        ref[:, 0:384] = dot(spread_out, saved).astype(ref.dtype)
    keep_ref[0:16, 384:512] = sums
    give_ref[:, 384:512] = jnp.concatenate([split_sums(sums)] * 8, axis=0)


def split_sums(sums):
    high = sums.astype(BF16).astype(F32)
    return jnp.where(left_half((16, 128)), high, sums - high).astype(BF16)


def merge_kernel(keep_ref, given_ref, out_ref):
    out_ref[:, 0:384] = (keep_ref[:, 0:384] + given_ref[:, 0:384].astype(F32)).astype(BF16)
    given = given_ref[0:16, 384:448].astype(F32) + given_ref[0:16, 448:512].astype(F32)
    sums = split_sums(keep_ref[0:16, 384:512] + jnp.concatenate([given, given], axis=1))
    for at in range(0, out_ref.shape[0], 16):
        out_ref[at : at + 16, 384:512] = sums


def scale_kernel(factor, part_ref, moved_ref, out_ref, grad_ref):
    total = part_ref[0:16, :].astype(F32)
    for at in range(16, part_ref.shape[0], 16):
        total = total + part_ref[at : at + 16, :].astype(F32)
    spread = (total[:, 384:385] + total[:, 448:449]) * (1.0 / (NTOK * 64)) + 1e-05
    grad = total[:, 0:384] * (factor / spread)
    grad = grad[0:8] + grad[8:16]
    pair = jnp.concatenate([grad, grad], axis=0).astype(BF16)
    for at in range(0, out_ref.shape[0], 16):
        out_ref[at : at + 16, :] = pair
    gap = guidance(moved_ref) - moved_ref[3].astype(F32)
    grad_ref[0] = gap[:, 64:128] / spread[0:1]
    grad_ref[1] = gap[:, 0:64] / spread[8:9]


def sum_kernel(part_ref, out_ref):
    total = part_ref[0:16, :].astype(F32)
    for at in range(16, part_ref.shape[0], 16):
        total = total + part_ref[at : at + 16, :].astype(F32)
    total = total[0:8] + total[8:16]
    pair = jnp.concatenate([total, total], axis=0).astype(BF16)
    for at in range(0, out_ref.shape[0], 16):
        out_ref[at : at + 16, :] = pair


def place_kernel(
    part_ref, prediction_ref, grad_ref, out_ref, prediction_out, grad_out, wide_ref, done
):
    stores = [
        pltpu.make_async_copy(prediction_ref, prediction_out, done.at[8]),
        pltpu.make_async_copy(grad_ref, grad_out, done.at[9]),
    ]
    for store in stores:
        store.start()
    at = 0
    for core in range(2):
        for g in range(4):
            lanes = pl.ds(768 * g + 384 * core, 384)
            for row in range(0, 64, 16):
                wide_ref[row : row + 16, lanes] = part_ref[at : at + 16, :].astype(F32)
                at += 16
            source, target = wide_ref.at[:, lanes], out_ref.at[:, lanes]
            stores.append(pltpu.make_async_copy(source, target, done.at[4 * core + g]))
            stores[-1].start()
    for store in stores:
        store.wait()


VECTOR = pl.BlockSpec(memory_space=pltpu.VMEM)


def params(mib):
    return pltpu.CompilerParams(vmem_limit_bytes=mib << 20)


def shape_of(shape, dtype):
    return jax.ShapeDtypeStruct(shape, dtype)


def fold(*operands):
    width = operands[3].shape[2]
    return pl.pallas_call(
        fold_kernel,
        out_shape=(
            pltpu.VMEM((ROWS, 128), BF16), pltpu.VMEM((64, 128), BF16), pltpu.VMEM((144, 128), F32)
        ),
        in_specs=[pl.BlockSpec(memory_space=pl.ANY)] * len(operands),
        out_specs=(VECTOR, VECTOR, VECTOR),
        scratch_shapes=[pltpu.VMEM(x.shape, x.dtype) for x in operands[:9]]
        + [
            pltpu.SMEM(operands[9].shape, jnp.int32),
            pltpu.VMEM((144, width // CHUNKS), BF16),
            pltpu.SemaphoreType.DMA((7 + 5 * CHUNKS,)),
        ],
        compiler_params=params(58),
        name="fold",
    )(*operands)


def attend(groups, *operands):
    heads = operands[3].shape[0]
    return pl.pallas_call(
        attend_kernel,
        out_shape=(shape_of((groups, 64, 128), BF16), pltpu.VMEM((1, 2, 64, 64), F32)),
        in_specs=[VECTOR] * 6,
        out_specs=(VECTOR, VECTOR),
        scratch_shapes=[
            pltpu.VMEM((64 * heads, 256), BF16),
            pltpu.VMEM((2, 64 * heads, 128), BF16),
            pltpu.VMEM((2, 64 * heads, 128), BF16),
        ],
        compiler_params=params(32),
        name="attend",
    )(*operands)


def per_device(
    noise_gen,
    noise_score,
    prev_latents,
    t_idx,
    w_in,
    w_qkv,
    w_out,
    w_final,
    mod_scale,
    mod_shift,
    saved_features,
):
    groups = lax.axis_size("group")
    heads = lax.axis_size("seq")
    copies = lax.axis_size("dp")
    width = w_in.shape[2]

    sent, own, local = fold(
        prev_latents, noise_gen, noise_score, w_in, mod_scale, mod_shift,
        w_out[0].T, w_final[0].T, w_qkv[0].transpose(1, 0, 2), t_idx,
    )
    everyone = lax.all_gather(sent, "seq", axis=0, tiled=True).reshape(heads, ROWS, 128)

    moved, prediction = attend(
        groups, noise_gen, noise_score, prev_latents, everyone, own, local
    )
    moved = lax.all_to_all(moved, "group", 0, 0, tiled=True)

    chips = heads // 2
    keep, give = pl.pallas_call(
        partial_kernel,
        out_shape=(pltpu.VMEM((16 * chips, 512), F32), shape_of((16 * chips, 512), BF16)),
        in_specs=[VECTOR] * 5,
        out_specs=(VECTOR, VECTOR),
        compiler_params=params(16),
        name="partial",
    )(moved, noise_score, prev_latents, local, saved_features)
    given = lax.ppermute(give, "seq", [(k, k ^ 1) for k in range(heads)])
    parts = pl.pallas_call(
        merge_kernel,
        out_shape=shape_of((16 * chips, 512), BF16),
        in_specs=[VECTOR] * 2,
        out_specs=VECTOR,
        compiler_params=params(16),
        name="merge",
    )(keep, given)
    same_part = [[2 * y + core for y in range(chips)] for core in range(2)]
    parts = lax.all_to_all(parts, "seq", 0, 0, tiled=True, axis_index_groups=same_part)

    factor = 1.0 / math.sqrt(2 * copies * NTOK)
    summed, dmd_grad = pl.pallas_call(
        lambda *refs: scale_kernel(factor, *refs),
        out_shape=(shape_of((copies * 8, 384), BF16), pltpu.VMEM((2, 64, 64), F32)),
        in_specs=[VECTOR] * 2,
        out_specs=(VECTOR, VECTOR),
        compiler_params=params(16),
        name="scale",
    )(parts, moved)
    summed = lax.all_to_all(summed, "dp", 0, 0, tiled=True)

    rows = pl.pallas_call(
        sum_kernel,
        out_shape=shape_of((groups * chips * 8, 384), BF16),
        in_specs=[VECTOR],
        out_specs=VECTOR,
        compiler_params=params(16),
        name="sum",
    )(summed)
    same_core = [
        [g * heads + 2 * y + core for g in range(groups) for y in range(chips)] for core in range(2)
    ]
    rows = lax.all_to_all(
        rows, ("group", "seq"), 0, 0, tiled=True, axis_index_groups=same_core
    )
    one_chip = [[2 * y, 2 * y + 1] for y in range(chips)]
    rows = lax.all_gather(rows, "seq", axis=0, tiled=True, axis_index_groups=one_chip)

    total, prediction, dmd_grad = pl.pallas_call(
        place_kernel,
        out_shape=(
            shape_of((64, width), F32), shape_of(prediction.shape, F32), shape_of(dmd_grad.shape, F32)
        ),
        in_specs=[VECTOR] * 3,
        out_specs=(pl.BlockSpec(memory_space=pl.ANY),) * 3,
        scratch_shapes=[pltpu.VMEM((64, width), F32), pltpu.SemaphoreType.DMA((10,))],
        compiler_params=params(16),
        name="place",
    )(rows, prediction, dmd_grad)
    return prediction, dmd_grad, total.T


def solution(mesh):
    placed = (
        P("dp", "seq", None),
        P("dp", "seq", None),
        P("dp", "seq", None),
        P("dp"),
        P("group", None, None),
        P("group", None, None, "seq"),
        P("group", "seq", None),
        P("group", None, None),
        P("group", None),
        P("group", None),
        P("dp", "seq", None),
    )
    return jax.shard_map(
        per_device,
        mesh=mesh,
        in_specs=placed,
        out_specs=(P("group", "dp", "seq", None), P("dp", "seq", None), P()),
        check_vma=False,
    )
```

```python
import math

import jax
import jax.numpy as jnp
from jax import lax
from jax.experimental import pallas as pl
from jax.experimental.pallas import tpu as pltpu
from jax.sharding import PartitionSpec as P

NTOK = 1024
NOISE_LEVEL_COUNT = 1000
BF16 = jnp.bfloat16
F32 = jnp.float32
CHUNKS = 3
ROWS = 208


def dot(a, b, lhs=1, rhs=0):
    return lax.dot_general(a, b, (((lhs,), (rhs,)), ((), ())), preferred_element_type=F32)


def left_half(shape):
    return lax.broadcasted_iota(jnp.int32, shape, 1) < 64


def levels(t_ref):
    gen = jnp.where(lax.axis_index("group") == 0, 1.0, 0.0).astype(F32)
    level = [(t_ref[i].astype(F32) + 0.5) * (1.0 / NOISE_LEVEL_COUNT) for i in range(2)]
    return gen, level, [gen + (1.0 - gen) * value for value in level]


def level_rows(local_ref, lanes):
    rows = [local_ref[k : k + 1, 0:lanes] for k in range(136, 141)]
    return rows[0], rows[1:3], rows[3:5]


def noisy_latent(level, prev, noise):
    return (1.0 - level) * prev + level * noise.astype(F32)


def fold_kernel(*refs):
    sources, (sent_ref, own_ref, local_ref), held = refs[:10], refs[10:13], refs[13:23]
    left_ref, arrived = refs[23:]
    t_ref = held[9]
    width = sources[3].shape[2]
    step = width // CHUNKS
    pairs = [(sources[k], held[k]) for k in (9, 0, 1, 2, 4, 5, 6)]
    for at in range(0, width, step):
        part = pl.ds(at, step)
        pairs.append((sources[3].at[:, :, part], held[3].at[:, :, part]))
        pairs.append((sources[7].at[:, part], held[7].at[:, part]))
        pairs += [(sources[8].at[c, part], held[8].at[c, part]) for c in range(3)]
    loads = [pltpu.make_async_copy(*pair, arrived.at[k]) for k, pair in enumerate(pairs)]
    for load in loads:
        load.start()
    prev_ref, gen_ref, noise_ref, w_in_ref, scale_ref, shift_ref = held[:6]
    w_out_ref, w_final_ref, w_qkv_ref = held[6:9]
    for load in loads[:7]:
        load.wait()
    gen, level, used = levels(t_ref)
    latents = []
    for i in range(2):
        noisy = noisy_latent(level[i], prev_ref[i], noise_ref[i])
        latents.append(gen * gen_ref[i].astype(F32) + (1.0 - gen) * noisy)
    latent = jnp.concatenate(latents, axis=0).astype(BF16)
    squares = jnp.zeros((128, 128), F32)
    final = jnp.zeros((144, 64), F32)
    folded = [jnp.zeros((144, 128), F32) for _ in range(3)]
    row = lax.broadcasted_iota(jnp.int32, (16, step), 0)
    for n in range(CHUNKS):
        at = n * step
        for load in loads[7 + 5 * n : 12 + 5 * n]:
            load.wait()
        part = w_in_ref[0, :, at : at + step]
        projected = dot(latent, part)
        for lane in range(0, step, 128):
            piece = projected[:, lane : lane + 128]
            squares = squares + piece * piece
        shift = shift_ref[:, at : at + step]
        high = shift.astype(BF16).astype(F32)
        shifts = jnp.where(row == 0, high, jnp.where(row == 1, shift - high, 0.0))
        scaled = part.astype(F32) * scale_ref[:, at : at + step]
        left_ref[0:64, :] = part
        left_ref[64:128, :] = scaled.astype(BF16)
        left_ref[128:144, :] = shifts.astype(BF16)
        final = final + dot(left_ref[...], w_final_ref[:, at : at + step], 1, 1)
        for c in range(3):
            folded[c] = folded[c] + dot(left_ref[...], w_qkv_ref[c, at : at + step, :])
    mean = jnp.sum(squares, axis=1, keepdims=True) * (1.0 / width)
    scaled = (latent.astype(F32) * lax.rsqrt(mean + 1e-06)).astype(BF16)
    own = jnp.concatenate([scaled[0:64], scaled[64:128]], axis=1)
    sent_ref[144:208, :] = own
    own_ref[...] = own
    q, k, v, f = [
        [part[0:64] + value * part[64:128] for value in used]
        for part in (*folded, jnp.concatenate([final, final], axis=1))
    ]
    q.append(jnp.broadcast_to(folded[0][128:129] + folded[0][129:130], (16, 128)))
    v.append(jnp.broadcast_to(folded[2][128:129] + folded[2][129:130], (16, 128)))
    q, k, v = [jnp.concatenate(part, axis=0).astype(BF16) for part in (q, k, v)]
    w_out = w_out_ref[...]
    scores = dot(q, k, 1, 1) * (math.log2(math.e) / math.sqrt(128.0))
    out = dot(v, jnp.concatenate([w_out, w_out], axis=0), 1, 1)
    left = left_half((64, 128))
    sent_ref[0:64, :] = jnp.where(left, scores[0:64], out[0:64]).astype(BF16)
    sent_ref[64:128, :] = jnp.where(left, out[64:128], scores[64:128]).astype(BF16)
    odd = lax.broadcasted_iota(jnp.int32, (16, 128), 0) > 0
    own_side = jnp.logical_xor(left_half((16, 128)), odd)
    sent_ref[128:144, :] = jnp.where(own_side, scores[128:144], out[128:144]).astype(BF16)
    local_ref[0:64, :] = f[0]
    local_ref[64:128, :] = f[1]
    both = final[128:129] + final[129:130]
    both = jnp.concatenate([both, both], axis=1)
    local_ref[128:136, :] = jnp.broadcast_to(both, (8, 128))
    for n, value in enumerate([gen, *level, *used]):
        local_ref[136 + n : 137 + n, :] = jnp.full((1, 128), value, F32)


def attend_kernel(
    gen_ref, noise_ref, prev_ref, all_ref, own_ref, local_ref,
    moved_ref, prediction_ref, keys_ref, query_ref, mixed_ref,
):
    heads = all_ref.shape[0]
    gen, level, used = level_rows(local_ref, 64)
    for s in range(heads):
        keys_ref[64 * s : 64 * s + 64, 0:128] = all_ref[s, 144:208, :]
    keys_ref[:, 128:256] = jnp.ones((64 * heads, 128), BF16)
    left = left_half((64, 128))
    own = own_ref[...].astype(F32)
    stacked = jnp.concatenate([jnp.where(left, own, 0.0), jnp.where(left, 0.0, own)], axis=0)
    stacked = stacked.astype(BF16)
    const_sum = jnp.zeros((16, 128), F32)
    for h in range(heads):
        block = all_ref[h, 0:128, :]
        const = all_ref[h, 128:144, :].astype(F32)
        const_sum = const_sum + const
        query = dot(stacked, block)
        rows = slice(64 * h, 64 * h + 64)
        query_ref[0, rows, :] = jnp.where(left, query[0:64] + const[0:1], 0.0).astype(BF16)
        query_ref[1, rows, :] = jnp.where(left, 0.0, query[64:128] + const[1:2]).astype(BF16)
    step = 256
    wide_left = left_half((step, 128))
    for i in range(2):
        for at in range(0, 64 * heads, step):
            rows = slice(at, at + step)
            scores = dot(query_ref[i, rows, :], keys_ref[:, 0:128], 1, 1)
            top = jnp.max(scores, axis=1, keepdims=True)
            weights = jnp.exp2(scores - top).astype(BF16)
            mixed = dot(weights, keys_ref[...])
            mixed = mixed[:, 0:128] / mixed[:, 128:256]
            keep = wide_left if i == 0 else jnp.logical_not(wide_left)
            mixed_ref[i, rows, :] = jnp.where(keep, mixed, 0.0).astype(BF16)
    total = dot(stacked, local_ref[0:128, :].astype(BF16))
    for h in range(heads):
        rows = slice(64 * h, 64 * h + 64)
        pair = jnp.concatenate([mixed_ref[0, rows, :], mixed_ref[1, rows, :]], axis=0)
        total = total + dot(pair, all_ref[h, 0:128, :])
    wide = level_rows(local_ref, 128)[2]
    first = wide[0] * (total[0:64] + const_sum[0:1] + local_ref[128:129, :])
    second = wide[1] * (total[64:128] + const_sum[1:2] + local_ref[128:129, :])
    moved = jnp.where(left, second, first)
    for g in range(moved_ref.shape[0]):
        moved_ref[g] = moved.astype(BF16)
    for i, part in ((0, moved[:, 64:128]), (1, moved[:, 0:64])):
        noisy = noisy_latent(level[i], prev_ref[i], noise_ref[i])
        prediction_ref[0, i] = gen * gen_ref[i].astype(F32) + (1.0 - gen) * noisy - part


def guidance(moved_ref):
    return 2.5 * moved_ref[1].astype(F32) - 1.5 * moved_ref[2].astype(F32)


def partial_kernel(moved_ref, noise_ref, prev_ref, local_ref, saved_ref, out_ref):
    level = level_rows(local_ref, 64)[1]
    guided = guidance(moved_ref)
    down = moved_ref[3].astype(F32) - guided
    halves = (slice(64, 128), slice(0, 64))
    row = lax.broadcasted_iota(jnp.int32, (16, 128), 0)
    sums = []
    for i in range(2):
        real = noisy_latent(level[i], prev_ref[i], noise_ref[i]) - guided[:, halves[i]]
        gap = jnp.abs(prev_ref[i] - real)
        sums.append(jnp.sum(jnp.sum(gap, axis=0, keepdims=True), axis=1, keepdims=True))
    sums = jnp.where(row < 8, sums[0], sums[1])
    high = sums.astype(BF16).astype(F32)
    sums = jnp.where(left_half((16, 128)), high, sums - high).astype(BF16)
    tokens = jnp.concatenate([down[:, halves[0]], down[:, halves[1]]], axis=0).astype(BF16)
    out_row = lax.broadcasted_iota(jnp.int32, (128, 64), 0)
    channel = lax.broadcasted_iota(jnp.int32, (128, 64), 1)
    pick = jnp.where((out_row // 16) * 8 + out_row % 8 == channel, 1.0, 0.0).astype(BF16)
    spread_out = dot(pick, tokens, 1, 1)
    image = (lax.broadcasted_iota(jnp.int32, (128, 128), 0) % 16) // 8
    owner = lax.broadcasted_iota(jnp.int32, (128, 128), 1) // 64
    spread_out = jnp.where(image == owner, spread_out, 0.0).astype(BF16)
    lanes = pl.ds(pl.multiple_of(lax.axis_index("group") * 768, 128), 768)
    saved = jnp.concatenate([saved_ref[0, :, lanes], saved_ref[1, :, lanes]], axis=0)
    grad = dot(spread_out, saved).astype(BF16)
    for a in range(8):
        for b in range(2):
            out_ref[2 * a + b, :, 0:384] = grad[16 * a : 16 * a + 16, 384 * b : 384 * b + 384]
            out_ref[2 * a + b, :, 384:512] = sums


def scale_kernel(factor, part_ref, moved_ref, out_ref, grad_ref):
    total = part_ref[0].astype(F32)
    for s in range(1, part_ref.shape[0]):
        total = total + part_ref[s].astype(F32)
    spread = (total[:, 384:385] + total[:, 448:449]) * (1.0 / (NTOK * 64)) + 1e-05
    grad = total[:, 0:384] * (factor / spread)
    grad = grad[0:8] + grad[8:16]
    pair = jnp.concatenate([grad, grad], axis=0).astype(BF16)
    for at in range(0, out_ref.shape[0], 16):
        out_ref[at : at + 16, :] = pair
    gap = guidance(moved_ref) - moved_ref[3].astype(F32)
    grad_ref[0] = gap[:, 64:128] / spread[0:1]
    grad_ref[1] = gap[:, 0:64] / spread[8:9]


def sum_kernel(part_ref, out_ref):
    total = part_ref[0:16, :].astype(F32)
    for at in range(16, part_ref.shape[0], 16):
        total = total + part_ref[at : at + 16, :].astype(F32)
    total = total[0:8] + total[8:16]
    pair = jnp.concatenate([total, total], axis=0).astype(BF16)
    for at in range(0, out_ref.shape[0], 16):
        out_ref[at : at + 16, :] = pair


def place_kernel(
    part_ref, prediction_ref, grad_ref, out_ref, prediction_out, grad_out, wide_ref, done
):
    stores = [
        pltpu.make_async_copy(prediction_ref, prediction_out, done.at[8]),
        pltpu.make_async_copy(grad_ref, grad_out, done.at[9]),
    ]
    for store in stores:
        store.start()
    at = 0
    for core in range(2):
        for g in range(4):
            lanes = pl.ds(768 * g + 384 * core, 384)
            for row in range(0, 64, 16):
                wide_ref[row : row + 16, lanes] = part_ref[at : at + 16, :].astype(F32)
                at += 16
            source, target = wide_ref.at[:, lanes], out_ref.at[:, lanes]
            stores.append(pltpu.make_async_copy(source, target, done.at[4 * core + g]))
            stores[-1].start()
    for store in stores:
        store.wait()


VECTOR = pl.BlockSpec(memory_space=pltpu.VMEM)


def params(mib):
    return pltpu.CompilerParams(vmem_limit_bytes=mib << 20)


def shape_of(shape, dtype):
    return jax.ShapeDtypeStruct(shape, dtype)


def fold(*operands):
    width = operands[3].shape[2]
    return pl.pallas_call(
        fold_kernel,
        out_shape=(
            pltpu.VMEM((ROWS, 128), BF16), pltpu.VMEM((64, 128), BF16), pltpu.VMEM((144, 128), F32)
        ),
        in_specs=[pl.BlockSpec(memory_space=pl.ANY)] * len(operands),
        out_specs=(VECTOR, VECTOR, VECTOR),
        scratch_shapes=[pltpu.VMEM(x.shape, x.dtype) for x in operands[:9]]
        + [
            pltpu.SMEM(operands[9].shape, jnp.int32),
            pltpu.VMEM((144, width // CHUNKS), BF16),
            pltpu.SemaphoreType.DMA((7 + 5 * CHUNKS,)),
        ],
        compiler_params=params(58),
        name="fold",
    )(*operands)


def attend(groups, *operands):
    heads = operands[3].shape[0]
    return pl.pallas_call(
        attend_kernel,
        out_shape=(shape_of((groups, 64, 128), BF16), pltpu.VMEM((1, 2, 64, 64), F32)),
        in_specs=[VECTOR] * 6,
        out_specs=(VECTOR, VECTOR),
        scratch_shapes=[
            pltpu.VMEM((64 * heads, 256), BF16),
            pltpu.VMEM((2, 64 * heads, 128), BF16),
            pltpu.VMEM((2, 64 * heads, 128), BF16),
        ],
        compiler_params=params(32),
        name="attend",
    )(*operands)


def per_device(
    noise_gen,
    noise_score,
    prev_latents,
    t_idx,
    w_in,
    w_qkv,
    w_out,
    w_final,
    mod_scale,
    mod_shift,
    saved_features,
):
    groups = lax.axis_size("group")
    heads = lax.axis_size("seq")
    copies = lax.axis_size("dp")
    width = w_in.shape[2]

    sent, own, local = fold(
        prev_latents, noise_gen, noise_score, w_in, mod_scale, mod_shift,
        w_out[0].T, w_final[0].T, w_qkv[0].transpose(1, 0, 2), t_idx,
    )
    everyone = lax.all_gather(sent, "seq", axis=0, tiled=True).reshape(heads, ROWS, 128)

    moved, prediction = attend(
        groups, noise_gen, noise_score, prev_latents, everyone, own, local
    )
    moved = lax.all_to_all(moved, "group", 0, 0, tiled=True)

    parts = pl.pallas_call(
        partial_kernel,
        out_shape=shape_of((heads, 16, 512), BF16),
        in_specs=[VECTOR] * 5,
        out_specs=VECTOR,
        compiler_params=params(16),
        name="partial",
    )(moved, noise_score, prev_latents, local, saved_features)
    parts = lax.all_to_all(parts, "seq", 0, 0, tiled=True)

    factor = 1.0 / math.sqrt(2 * copies * NTOK)
    summed, dmd_grad = pl.pallas_call(
        lambda *refs: scale_kernel(factor, *refs),
        out_shape=(shape_of((copies * 8, 384), BF16), pltpu.VMEM((2, 64, 64), F32)),
        in_specs=[VECTOR] * 2,
        out_specs=(VECTOR, VECTOR),
        compiler_params=params(16),
        name="scale",
    )(parts, moved)
    summed = lax.all_to_all(summed, "dp", 0, 0, tiled=True)

    chips = heads // 2
    rows = pl.pallas_call(
        sum_kernel,
        out_shape=shape_of((groups * chips * 8, 384), BF16),
        in_specs=[VECTOR],
        out_specs=VECTOR,
        compiler_params=params(16),
        name="sum",
    )(summed)
    same_core = [
        [g * heads + 2 * y + core for g in range(groups) for y in range(chips)] for core in range(2)
    ]
    rows = lax.all_to_all(
        rows, ("group", "seq"), 0, 0, tiled=True, axis_index_groups=same_core
    )
    one_chip = [[2 * y, 2 * y + 1] for y in range(chips)]
    rows = lax.all_gather(rows, "seq", axis=0, tiled=True, axis_index_groups=one_chip)

    total, prediction, dmd_grad = pl.pallas_call(
        place_kernel,
        out_shape=(
            shape_of((64, width), F32), shape_of(prediction.shape, F32), shape_of(dmd_grad.shape, F32)
        ),
        in_specs=[VECTOR] * 3,
        out_specs=(pl.BlockSpec(memory_space=pl.ANY),) * 3,
        scratch_shapes=[pltpu.VMEM((64, width), F32), pltpu.SemaphoreType.DMA((10,))],
        compiler_params=params(16),
        name="place",
    )(rows, prediction, dmd_grad)
    return prediction, dmd_grad, total.T


def solution(mesh):
    placed = (
        P("dp", "seq", None),
        P("dp", "seq", None),
        P("dp", "seq", None),
        P("dp"),
        P("group", None, None),
        P("group", None, None, "seq"),
        P("group", "seq", None),
        P("group", None, None),
        P("group", None),
        P("group", None),
        P("dp", "seq", None),
    )
    return jax.shard_map(
        per_device,
        mesh=mesh,
        in_specs=placed,
        out_specs=(P("group", "dp", "seq", None), P("dp", "seq", None), P()),
        check_vma=False,
    )
```

```python
import math

import jax
import jax.numpy as jnp
from jax import lax
from jax.experimental import pallas as pl
from jax.experimental.pallas import tpu as pltpu
from jax.sharding import PartitionSpec as P

NTOK = 1024
NOISE_LEVEL_COUNT = 1000
BF16 = jnp.bfloat16
F32 = jnp.float32
CHUNKS = 3
ROWS = 208


def dot(a, b, lhs=1, rhs=0):
    return lax.dot_general(a, b, (((lhs,), (rhs,)), ((), ())), preferred_element_type=F32)


def left_half(shape):
    return lax.broadcasted_iota(jnp.int32, shape, 1) < 64


def levels(t_ref):
    gen = jnp.where(lax.axis_index("group") == 0, 1.0, 0.0).astype(F32)
    level = [(t_ref[i].astype(F32) + 0.5) * (1.0 / NOISE_LEVEL_COUNT) for i in range(2)]
    return gen, level, [gen + (1.0 - gen) * value for value in level]


def level_rows(local_ref, lanes):
    rows = [local_ref[k : k + 1, 0:lanes] for k in range(136, 141)]
    return rows[0], rows[1:3], rows[3:5]


def noisy_latent(level, prev, noise):
    return (1.0 - level) * prev + level * noise.astype(F32)


def fold_kernel(*refs):
    sources, (sent_ref, own_ref, local_ref), held = refs[:10], refs[10:13], refs[13:23]
    left_ref, arrived = refs[23:]
    t_ref = held[9]
    width = sources[3].shape[2]
    step = width // CHUNKS
    pairs = [(sources[k], held[k]) for k in (9, 0, 1, 2, 4, 5, 6)]
    for at in range(0, width, step):
        part = pl.ds(at, step)
        pairs.append((sources[3].at[:, :, part], held[3].at[:, :, part]))
        pairs.append((sources[7].at[:, part], held[7].at[:, part]))
        pairs += [(sources[8].at[c, part], held[8].at[c, part]) for c in range(3)]
    loads = [pltpu.make_async_copy(*pair, arrived.at[k]) for k, pair in enumerate(pairs)]
    for load in loads:
        load.start()
    prev_ref, gen_ref, noise_ref, w_in_ref, scale_ref, shift_ref = held[:6]
    w_out_ref, w_final_ref, w_qkv_ref = held[6:9]
    for load in loads[:7]:
        load.wait()
    gen, level, used = levels(t_ref)
    latents = []
    for i in range(2):
        noisy = noisy_latent(level[i], prev_ref[i], noise_ref[i])
        latents.append(gen * gen_ref[i].astype(F32) + (1.0 - gen) * noisy)
    latent = jnp.concatenate(latents, axis=0).astype(BF16)
    squares = jnp.zeros((128, 128), F32)
    final = jnp.zeros((144, 64), F32)
    folded = [jnp.zeros((144, 128), F32) for _ in range(3)]
    row = lax.broadcasted_iota(jnp.int32, (16, step), 0)
    for n in range(CHUNKS):
        at = n * step
        for load in loads[7 + 5 * n : 12 + 5 * n]:
            load.wait()
        part = w_in_ref[0, :, at : at + step]
        projected = dot(latent, part)
        for lane in range(0, step, 128):
            piece = projected[:, lane : lane + 128]
            squares = squares + piece * piece
        shift = shift_ref[:, at : at + step]
        high = shift.astype(BF16).astype(F32)
        shifts = jnp.where(row == 0, high, jnp.where(row == 1, shift - high, 0.0))
        scaled = part.astype(F32) * scale_ref[:, at : at + step]
        left_ref[0:64, :] = part
        left_ref[64:128, :] = scaled.astype(BF16)
        left_ref[128:144, :] = shifts.astype(BF16)
        final = final + dot(left_ref[...], w_final_ref[:, at : at + step], 1, 1)
        for c in range(3):
            folded[c] = folded[c] + dot(left_ref[...], w_qkv_ref[c, at : at + step, :])
    mean = jnp.sum(squares, axis=1, keepdims=True) * (1.0 / width)
    scaled = (latent.astype(F32) * lax.rsqrt(mean + 1e-06)).astype(BF16)
    own = jnp.concatenate([scaled[0:64], scaled[64:128]], axis=1)
    sent_ref[144:208, :] = own
    own_ref[...] = own
    q, k, v, f = [
        [part[0:64] + value * part[64:128] for value in used]
        for part in (*folded, jnp.concatenate([final, final], axis=1))
    ]
    q.append(jnp.broadcast_to(folded[0][128:129] + folded[0][129:130], (16, 128)))
    v.append(jnp.broadcast_to(folded[2][128:129] + folded[2][129:130], (16, 128)))
    q, k, v = [jnp.concatenate(part, axis=0).astype(BF16) for part in (q, k, v)]
    w_out = w_out_ref[...]
    scores = dot(q, k, 1, 1) * (math.log2(math.e) / math.sqrt(128.0))
    out = dot(v, jnp.concatenate([w_out, w_out], axis=0), 1, 1)
    left = left_half((64, 128))
    sent_ref[0:64, :] = jnp.where(left, scores[0:64], out[0:64]).astype(BF16)
    sent_ref[64:128, :] = jnp.where(left, out[64:128], scores[64:128]).astype(BF16)
    odd = lax.broadcasted_iota(jnp.int32, (16, 128), 0) > 0
    own_side = jnp.logical_xor(left_half((16, 128)), odd)
    sent_ref[128:144, :] = jnp.where(own_side, scores[128:144], out[128:144]).astype(BF16)
    local_ref[0:64, :] = f[0]
    local_ref[64:128, :] = f[1]
    both = final[128:129] + final[129:130]
    both = jnp.concatenate([both, both], axis=1)
    local_ref[128:136, :] = jnp.broadcast_to(both, (8, 128))
    for n, value in enumerate([gen, *level, *used]):
        local_ref[136 + n : 137 + n, :] = jnp.full((1, 128), value, F32)


def attend_kernel(
    gen_ref, noise_ref, prev_ref, all_ref, own_ref, local_ref,
    moved_ref, prediction_ref, keys_ref, query_ref, mixed_ref,
):
    heads = all_ref.shape[0]
    gen, level, used = level_rows(local_ref, 64)
    for s in range(heads):
        keys_ref[64 * s : 64 * s + 64, 0:128] = all_ref[s, 144:208, :]
    keys_ref[:, 128:256] = jnp.ones((64 * heads, 128), BF16)
    left = left_half((64, 128))
    own = own_ref[...].astype(F32)
    stacked = jnp.concatenate([jnp.where(left, own, 0.0), jnp.where(left, 0.0, own)], axis=0)
    stacked = stacked.astype(BF16)
    const_sum = jnp.zeros((16, 128), F32)
    for h in range(heads):
        block = all_ref[h, 0:128, :]
        const = all_ref[h, 128:144, :].astype(F32)
        const_sum = const_sum + const
        query = dot(stacked, block)
        rows = slice(64 * h, 64 * h + 64)
        query_ref[0, rows, :] = jnp.where(left, query[0:64] + const[0:1], 0.0).astype(BF16)
        query_ref[1, rows, :] = jnp.where(left, 0.0, query[64:128] + const[1:2]).astype(BF16)
    step = 256
    wide_left = left_half((step, 128))
    for i in range(2):
        for at in range(0, 64 * heads, step):
            rows = slice(at, at + step)
            scores = dot(query_ref[i, rows, :], keys_ref[:, 0:128], 1, 1)
            top = jnp.max(scores, axis=1, keepdims=True)
            weights = jnp.exp2(scores - top).astype(BF16)
            mixed = dot(weights, keys_ref[...])
            mixed = mixed[:, 0:128] / mixed[:, 128:256]
            keep = wide_left if i == 0 else jnp.logical_not(wide_left)
            mixed_ref[i, rows, :] = jnp.where(keep, mixed, 0.0).astype(BF16)
    total = dot(stacked, local_ref[0:128, :].astype(BF16))
    for h in range(heads):
        rows = slice(64 * h, 64 * h + 64)
        pair = jnp.concatenate([mixed_ref[0, rows, :], mixed_ref[1, rows, :]], axis=0)
        total = total + dot(pair, all_ref[h, 0:128, :])
    wide = level_rows(local_ref, 128)[2]
    first = wide[0] * (total[0:64] + const_sum[0:1] + local_ref[128:129, :])
    second = wide[1] * (total[64:128] + const_sum[1:2] + local_ref[128:129, :])
    moved = jnp.where(left, second, first)
    for g in range(moved_ref.shape[0]):
        moved_ref[g] = moved.astype(BF16)
    for i, part in ((0, moved[:, 64:128]), (1, moved[:, 0:64])):
        noisy = noisy_latent(level[i], prev_ref[i], noise_ref[i])
        prediction_ref[0, i] = gen * gen_ref[i].astype(F32) + (1.0 - gen) * noisy - part


def guidance(moved_ref):
    return 2.5 * moved_ref[1].astype(F32) - 1.5 * moved_ref[2].astype(F32)


def partial_kernel(moved_ref, noise_ref, prev_ref, local_ref, saved_ref, out_ref):
    level = level_rows(local_ref, 64)[1]
    guided = guidance(moved_ref)
    down = moved_ref[3].astype(F32) - guided
    halves = (slice(64, 128), slice(0, 64))
    row = lax.broadcasted_iota(jnp.int32, (8, 128), 0)
    sums = []
    for i in range(2):
        real = noisy_latent(level[i], prev_ref[i], noise_ref[i]) - guided[:, halves[i]]
        gap = jnp.abs(prev_ref[i] - real)
        sums.append(jnp.sum(jnp.sum(gap, axis=0, keepdims=True), axis=1, keepdims=True))
    sums = jnp.where(row < 4, sums[0], sums[1])
    high = sums.astype(BF16).astype(F32)
    sums = jnp.where(left_half((8, 128)), high, sums - high).astype(BF16)
    tokens = jnp.concatenate([down[:, halves[0]], down[:, halves[1]]], axis=0).astype(BF16)
    out_row = lax.broadcasted_iota(jnp.int32, (128, 64), 0)
    channel = lax.broadcasted_iota(jnp.int32, (128, 64), 1)
    pick = jnp.where((out_row // 16) * 8 + out_row % 8 == channel, 1.0, 0.0).astype(BF16)
    spread_out = dot(pick, tokens, 1, 1)
    image = (lax.broadcasted_iota(jnp.int32, (128, 128), 0) % 16) // 8
    owner = lax.broadcasted_iota(jnp.int32, (128, 128), 1) // 64
    spread_out = jnp.where(image == owner, spread_out, 0.0).astype(BF16)
    lanes = pl.ds(pl.multiple_of(lax.axis_index("group") * 768, 128), 768)
    saved = jnp.concatenate([saved_ref[0, :, lanes], saved_ref[1, :, lanes]], axis=0)
    grad = dot(spread_out, saved).astype(BF16)
    for a in range(8):
        for b in range(2):
            for k in range(3):
                lane = 384 * b + 128 * k
                part = grad[16 * a : 16 * a + 16, lane : lane + 128]
                out_ref[2 * a + b, 16 * k : 16 * k + 16, :] = part
            out_ref[2 * a + b, 48:56, :] = sums


def scale_kernel(factor, part_ref, moved_ref, out_ref, grad_ref):
    total = part_ref[0].astype(F32)
    for s in range(1, part_ref.shape[0]):
        total = total + part_ref[s].astype(F32)
    spread = (total[48:56, 0:1] + total[48:56, 64:65]) * (1.0 / (NTOK * 64)) + 1e-05
    grad = jnp.concatenate([total[0:16], total[16:32], total[32:48]], axis=1)
    grad = grad[0:8] * (factor / spread[0:1]) + grad[8:16] * (factor / spread[4:5])
    pair = jnp.concatenate([grad, grad], axis=0).astype(BF16)
    for at in range(0, out_ref.shape[0], 16):
        out_ref[at : at + 16, :] = pair
    gap = guidance(moved_ref) - moved_ref[3].astype(F32)
    grad_ref[0] = gap[:, 64:128] / spread[0:1]
    grad_ref[1] = gap[:, 0:64] / spread[4:5]


def sum_kernel(part_ref, out_ref):
    total = part_ref[0:16, :].astype(F32)
    for at in range(16, part_ref.shape[0], 16):
        total = total + part_ref[at : at + 16, :].astype(F32)
    total = total[0:8] + total[8:16]
    pair = jnp.concatenate([total, total], axis=0).astype(BF16)
    for at in range(0, out_ref.shape[0], 16):
        out_ref[at : at + 16, :] = pair


def place_kernel(
    part_ref, prediction_ref, grad_ref, out_ref, prediction_out, grad_out, wide_ref, done
):
    stores = [
        pltpu.make_async_copy(prediction_ref, prediction_out, done.at[8]),
        pltpu.make_async_copy(grad_ref, grad_out, done.at[9]),
    ]
    for store in stores:
        store.start()
    at = 0
    for core in range(2):
        for g in range(4):
            lanes = pl.ds(768 * g + 384 * core, 384)
            for row in range(0, 64, 16):
                wide_ref[row : row + 16, lanes] = part_ref[at : at + 16, :].astype(F32)
                at += 16
            source, target = wide_ref.at[:, lanes], out_ref.at[:, lanes]
            stores.append(pltpu.make_async_copy(source, target, done.at[4 * core + g]))
            stores[-1].start()
    for store in stores:
        store.wait()


VECTOR = pl.BlockSpec(memory_space=pltpu.VMEM)


def params(mib):
    return pltpu.CompilerParams(vmem_limit_bytes=mib << 20)


def shape_of(shape, dtype):
    return jax.ShapeDtypeStruct(shape, dtype)


def fold(*operands):
    width = operands[3].shape[2]
    return pl.pallas_call(
        fold_kernel,
        out_shape=(
            pltpu.VMEM((ROWS, 128), BF16), pltpu.VMEM((64, 128), BF16), pltpu.VMEM((144, 128), F32)
        ),
        in_specs=[pl.BlockSpec(memory_space=pl.ANY)] * len(operands),
        out_specs=(VECTOR, VECTOR, VECTOR),
        scratch_shapes=[pltpu.VMEM(x.shape, x.dtype) for x in operands[:9]]
        + [
            pltpu.SMEM(operands[9].shape, jnp.int32),
            pltpu.VMEM((144, width // CHUNKS), BF16),
            pltpu.SemaphoreType.DMA((7 + 5 * CHUNKS,)),
        ],
        compiler_params=params(58),
        name="fold",
    )(*operands)


def attend(groups, *operands):
    heads = operands[3].shape[0]
    return pl.pallas_call(
        attend_kernel,
        out_shape=(shape_of((groups, 64, 128), BF16), pltpu.VMEM((1, 2, 64, 64), F32)),
        in_specs=[VECTOR] * 6,
        out_specs=(VECTOR, VECTOR),
        scratch_shapes=[
            pltpu.VMEM((64 * heads, 256), BF16),
            pltpu.VMEM((2, 64 * heads, 128), BF16),
            pltpu.VMEM((2, 64 * heads, 128), BF16),
        ],
        compiler_params=params(32),
        name="attend",
    )(*operands)


def per_device(
    noise_gen,
    noise_score,
    prev_latents,
    t_idx,
    w_in,
    w_qkv,
    w_out,
    w_final,
    mod_scale,
    mod_shift,
    saved_features,
):
    groups = lax.axis_size("group")
    heads = lax.axis_size("seq")
    copies = lax.axis_size("dp")
    width = w_in.shape[2]

    sent, own, local = fold(
        prev_latents, noise_gen, noise_score, w_in, mod_scale, mod_shift,
        w_out[0].T, w_final[0].T, w_qkv[0].transpose(1, 0, 2), t_idx,
    )
    everyone = lax.all_gather(sent, "seq", axis=0, tiled=True).reshape(heads, ROWS, 128)

    moved, prediction = attend(
        groups, noise_gen, noise_score, prev_latents, everyone, own, local
    )
    moved = lax.all_to_all(moved, "group", 0, 0, tiled=True)

    parts = pl.pallas_call(
        partial_kernel,
        out_shape=shape_of((heads, 56, 128), BF16),
        in_specs=[VECTOR] * 5,
        out_specs=VECTOR,
        compiler_params=params(16),
        name="partial",
    )(moved, noise_score, prev_latents, local, saved_features)
    parts = lax.all_to_all(parts, "seq", 0, 0, tiled=True)

    factor = 1.0 / math.sqrt(2 * copies * NTOK)
    summed, dmd_grad = pl.pallas_call(
        lambda *refs: scale_kernel(factor, *refs),
        out_shape=(shape_of((copies * 8, 384), BF16), pltpu.VMEM((2, 64, 64), F32)),
        in_specs=[VECTOR] * 2,
        out_specs=(VECTOR, VECTOR),
        compiler_params=params(16),
        name="scale",
    )(parts, moved)
    summed = lax.all_to_all(summed, "dp", 0, 0, tiled=True)

    chips = heads // 2
    rows = pl.pallas_call(
        sum_kernel,
        out_shape=shape_of((groups * chips * 8, 384), BF16),
        in_specs=[VECTOR],
        out_specs=VECTOR,
        compiler_params=params(16),
        name="sum",
    )(summed)
    same_core = [
        [g * heads + 2 * y + core for g in range(groups) for y in range(chips)] for core in range(2)
    ]
    rows = lax.all_to_all(
        rows, ("group", "seq"), 0, 0, tiled=True, axis_index_groups=same_core
    )
    one_chip = [[2 * y, 2 * y + 1] for y in range(chips)]
    rows = lax.all_gather(rows, "seq", axis=0, tiled=True, axis_index_groups=one_chip)

    total, prediction, dmd_grad = pl.pallas_call(
        place_kernel,
        out_shape=(
            shape_of((64, width), F32), shape_of(prediction.shape, F32), shape_of(dmd_grad.shape, F32)
        ),
        in_specs=[VECTOR] * 3,
        out_specs=(pl.BlockSpec(memory_space=pl.ANY),) * 3,
        scratch_shapes=[pltpu.VMEM((64, width), F32), pltpu.SemaphoreType.DMA((10,))],
        compiler_params=params(16),
        name="place",
    )(rows, prediction, dmd_grad)
    return prediction, dmd_grad, total.T


def solution(mesh):
    placed = (
        P("dp", "seq", None),
        P("dp", "seq", None),
        P("dp", "seq", None),
        P("dp"),
        P("group", None, None),
        P("group", None, None, "seq"),
        P("group", "seq", None),
        P("group", None, None),
        P("group", None),
        P("group", None),
        P("dp", "seq", None),
    )
    return jax.shard_map(
        per_device,
        mesh=mesh,
        in_specs=placed,
        out_specs=(P("group", "dp", "seq", None), P("dp", "seq", None), P()),
        check_vma=False,
    )
```
